512 devices in a mesh: hid: 32 (over y, z_lo), col: 16 (over x, z_hi, core).
Axes of the slice: x: 4, y: 8, z: 8 (z_hi: 2, z_lo: 4; z = z_hi * 4 + z_lo), core: 2. Of those that a mesh axis runs over, the one named last changes fastest.
Arguments:
- inputs: bfloat16 [15360, 28672], P('col', 'hid'), may hold values from -6 to 6
- out_grads: bfloat16 [15360, 8192], P('col', 'hid'), may hold values from -6 to 6
- proj_in: bfloat16 [96, 28672], P(None, 'hid'), may hold values from -0.03125 to 0.03125
- proj_out: bfloat16 [192, 8192], P(None, 'hid'), may hold values from -0.0625 to 0.0625
- curvature: bfloat16 [18432, 18432], P('hid', 'col'), may hold values from -0.119628906 to 0.119628906
Outputs:
- applied: float32 [480, 18432], P('hid', 'col')
- curvature_new: bfloat16 [18432, 18432], P('hid', 'col')
The draws below stay inside these ranges and needn't reach their ends.
All inputs are finite; a program needn't handle non-finite values.
Results may differ from the reference program's by a relative error of at most 0.012.
Values may be sent and summed in bfloat16 or wider, within the bound.
A program may use at most 64 MiB of HBM per device.

```python
import jax
import jax.numpy as jnp
from jax import lax

HIDDEN_SIZE = 28672
DMODEL = 8192
PIN = 96
POUT = 192
SEQ = 32
RANK = 18432
TOKENS = 15360
N_HID = 32


def block_scale(own_key, shape, shards, least, high):
    factor_of = 1.0
    for position, shards_of in shards:
        draws = jax.random.uniform(jax.random.fold_in(jax.random.fold_in(own_key, 6), position), (shards_of,), jnp.float32, least / len(shards), high / len(shards))
        factor_of = factor_of * jnp.repeat(jnp.exp(draws), shape[position] // shards_of).reshape((-1,) + (1,) * (len(shape) - 1 - position))
    return factor_of


def noise(key, dims, spread, bound, cuts=(), kind=jnp.bfloat16):
    array = jax.random.normal(key, dims, jnp.float32) * spread
    if len(cuts) > 0:
        array = block_scale(key, dims, cuts, -0.22, 0.18) * array
    return jnp.clip(array, min=-bound, max=bound).astype(kind)


def setup_inputs(seed: int = 0) -> dict:
    streams_of = jax.random.split(jax.random.key(seed), 6)
    inputs = noise(streams_of[0], (TOKENS, HIDDEN_SIZE), 1.0, 6.0, ((0, 16), (1, 32)))
    out_grads = noise(streams_of[1], (TOKENS, DMODEL), 1.0, 6.0, ((0, 16), (1, 32)))
    proj_in = noise(streams_of[2], (PIN, HIDDEN_SIZE), HIDDEN_SIZE ** -0.5, 0.03125, ((1, 32),))
    proj_out = noise(streams_of[3], (POUT, DMODEL), DMODEL ** -0.5, 0.0625, ((1, 32),))
    curvature = noise(streams_of[4], (RANK, RANK), 0.02, 0.119628906, ((0, 32), (1, 16)))
    return dict(inputs=inputs, out_grads=out_grads, proj_in=proj_in, proj_out=proj_out, curvature=curvature)


gram_weight = 1.0 / 64.0
apply_weight = 1.0 / 16.0


def reference(inputs, out_grads, proj_in, proj_out, curvature):
    contract = (((1,), (1,)), ((), ()))
    feat = lax.dot_general(inputs, proj_in, contract, preferred_element_type=jnp.float32).astype(jnp.bfloat16)
    grad = lax.dot_general(out_grads, proj_out, contract, preferred_element_type=jnp.float32).astype(jnp.bfloat16)
    examples = feat.shape[0] // SEQ
    rows = jnp.einsum("eti,etj->eij", feat.reshape(examples, SEQ, PIN).astype(jnp.float32), grad.reshape(examples, SEQ, POUT).astype(jnp.float32))
    rows = rows.reshape(examples, RANK).astype(jnp.bfloat16)
    width = RANK // N_HID
    factor = gram_weight / examples

    def step(total, index):
        start = (index * width).astype(jnp.int32)
        left = lax.dynamic_slice_in_dim(rows, start, width, 1)
        stored = lax.dynamic_slice_in_dim(curvature, start, width, 0)
        gram = lax.dot_general(left, rows, (((0,), (0,)), ((), ())), preferred_element_type=jnp.float32)
        updated = (stored.astype(jnp.float32) + gram * factor).astype(jnp.bfloat16)
        total = total + jnp.dot(left, updated, preferred_element_type=jnp.float32)
        return total, updated

    total, blocks = lax.scan(step, jnp.zeros((examples, RANK), jnp.float32), jnp.arange(N_HID, dtype=jnp.int32))
    return total * apply_weight, blocks.reshape(RANK, RANK)
```

```python
import jax
import jax.numpy as jnp
from jax import lax
from jax.experimental import pallas as pl
from jax.experimental.pallas import tpu as pltpu
from jax.sharding import PartitionSpec as P

MESH = pl.DeviceIdType.MESH
F32 = jnp.float32
BF16 = jnp.bfloat16

PIN = 96
POUT = 192
FEATS = PIN + POUT
SEQ = 32
EXAMPLES = 480
NY, NZ = 8, 4
N_HID, N_COL = 32, 16
OWN = 15
TOK = OWN * SEQ
NW = 1152
KW = 576
KP = 640
gram_weight = 1.0 / 64.0
apply_weight = 1.0 / 16.0
NT = (((1,), (1,)), ((), ()))


def slot_of(y, z):
    return (z // 2) * 16 + y * 2 + z % 2


def kernel(
    x_hbm, g_hbm, wi_hbm, wo_hbm, c_hbm,
    app_ref, cn_hbm,
    xv, gv, wiv, wov, cv,
    part, r1, s1, r2, s2, r3, featv, ge, go, rows,
    rn, rk, rkt, cn, p, rp, zs, zr,
    in_sem, a1s, a1r, a2s, a2r, a3s, a3r, ns, nr, ks, kr,
    zas, zar, yas, yar, khs, khr, kxs, kxr, kcs, kcr,
    rps, rpr, zrs, zrr, out_sem,
):
    h = lax.axis_index("hid")
    c = lax.axis_index("col")
    y, z = h // NZ, h % NZ
    core = c % 2
    m = c // 2
    x, zh = m // 2, m % 2
    half = z % 2
    is_target = z == 2 * core + y // 4
    is_root = jnp.logical_and(y == m, core == z // 2)
    own_slot = slot_of(y, z)

    def hid_dev(yy, zz):
        return (yy * NZ + zz, c)

    def col_dev(cc):
        return (h, cc)

    def send(src, dst, ssem, rsem, dev):
        copy = pltpu.make_async_remote_copy(
            src_ref=src, dst_ref=dst, send_sem=ssem, recv_sem=rsem,
            device_id=dev, device_id_type=MESH,
        )
        copy.start()

    def wait_for(ref, sem):
        pltpu.make_async_copy(ref, ref, sem).wait()

    loads = []
    for i, (src, dst) in enumerate(
        ((x_hbm, xv), (wi_hbm, wiv), (g_hbm, gv), (wo_hbm, wov), (c_hbm, cv))
    ):
        load = pltpu.make_async_copy(src, dst, in_sem.at[i])
        load.start()
        loads.append(load)

    barrier = pltpu.get_barrier_semaphore()

    def greet(dev):
        pl.semaphore_signal(barrier, inc=1, device_id=dev, device_id_type=MESH)

    for d in range(1, NY):
        greet(hid_dev((y + d) % NY, z))
    for d in range(1, NZ):
        greet(hid_dev(y, (z + d) % NZ))
    zh_c = (x * 2 + (1 - zh)) * 2 + core
    greet(col_dev(zh_c))
    for d in range(1, 4):
        greet(col_dev((((x + d) % 4) * 2 + zh) * 2 + core))
    greet(col_dev(m * 2 + 1 - core))

    @pl.when(jnp.logical_not(is_root))
    def _():
        greet(col_dev(h // 2))

    zero_tail = jnp.zeros((FEATS, 128), BF16)
    for hf in range(2):
        part[4 * hf + 3] = zero_tail
    loads[2].wait()
    loads[3].wait()

    def project(w, v, first):
        for hf in range(2):
            t = lax.dot_general(
                w[...], v[TOK * hf : TOK * (hf + 1), :], NT, preferred_element_type=F32
            ).astype(BF16)
            n = t.shape[0]
            for q in range(3):
                part[4 * hf + q, first : first + n, :] = t[:, 128 * q : 128 * (q + 1)]
            part[4 * hf + 3, first : first + n, 0:96] = t[:, 384:480]

    project(wov, gv, 0)
    loads[0].wait()
    loads[1].wait()
    project(wiv, xv, POUT)

    pl.semaphore_wait(barrier, jnp.where(is_root, 30, 15))

    for d in (4, 3, 5, 2, 6, 1, 7):
        yy = (y + d) % NY
        send(part.at[yy], r1.at[d - 1], a1s, a1r, hid_dev(yy, z))
    parity_zero = jnp.zeros((64, NW), BF16)
    cn[pl.ds(pl.multiple_of(KW * (1 - h % 2), 64), 64), :] = parity_zero
    wait_for(r1, a1r)
    total = part[y].astype(F32)
    for d in range(7):
        total = total + r1[d].astype(F32)
    s1[...] = total.astype(BF16)

    z_target = 2 * core + y // 4

    @pl.when(jnp.logical_not(is_target))
    def _():
        send(s1, r2.at[(z - z_target + NZ) % NZ - 1], a2s, a2r, hid_dev(y, z_target))
        wait_for(s1, a2s)

    @pl.when(is_target)
    def _():
        wait_for(r2, a2r)
        whole = s1[...].astype(F32)
        for d in range(3):
            whole = whole + r2[d].astype(F32)
        s2[...] = whole.astype(BF16)
        place = r3.at[:, pl.ds(pl.multiple_of(128 * (y % 4), 128), 128)]

        @pl.when(y != m)
        def _():
            send(s2, place, a3s, a3r, hid_dev(m, z))
            wait_for(s2, a3s)

        @pl.when(y == m)
        def _():
            pltpu.make_async_copy(s2, place, a3r).start()

    k_base = core * 16 + m * 2

    @pl.when(is_root)
    def _():
        wait_for(r3, a3r)
        ge[0:POUT, :] = r3[0:POUT, :]
        ge[POUT:256, :] = jnp.zeros((64, 512), BF16)
        go[0:64, :] = jnp.zeros((64, 512), BF16)
        go[64:256, :] = r3[0:POUT, :]
        featv[...] = r3[POUT:FEATS, :].astype(F32)
        mine = (
            lax.broadcasted_iota(jnp.int32, (16, 512), 1) // SEQ
            == lax.broadcasted_iota(jnp.int32, (16, 512), 0)
        )

        def form(i, carry):
            def spread(odd):
                return jnp.concatenate(
                    [
                        jnp.where(
                            mine,
                            jnp.broadcast_to(featv[pl.ds(i * 24 + 2 * q + odd, 1), :], (16, 512)),
                            0.0,
                        ).astype(BF16)
                        for q in range(12)
                    ],
                    axis=0,
                )

            even = lax.dot_general(spread(0), ge[...], NT, preferred_element_type=F32)
            odd = lax.dot_general(spread(1), go[...], NT, preferred_element_type=F32)
            for q in range(12):
                e = even[16 * q : 16 * (q + 1)]
                o = odd[16 * q : 16 * (q + 1)]
                three = jnp.concatenate(
                    [e[:, 0:128], e[:, 128:256] + o[:, 0:128], o[:, 128:256]], axis=1
                )
                at = pl.multiple_of(i * 4608 + 384 * q, 128)
                rows[:, pl.ds(at, 384)] = three.astype(BF16)
            return carry

        lax.fori_loop(0, 4, form, 0)

        def n_slice(cc):
            return rows.at[:, pl.ds(pl.multiple_of(cc * NW, 128), NW)]

        def k_slice(kk):
            return rows.at[:, pl.ds(pl.multiple_of((kk // 2) * NW + (kk % 2) * 512, 128), KP)]

        pltpu.make_async_copy(n_slice(c), rn.at[own_slot], nr).start()
        pltpu.make_async_copy(k_slice(h), rk.at[own_slot], kr).start()

        def to_col(d, carry):
            cc = (c + d) % N_COL
            send(n_slice(cc), rn.at[own_slot], ns, nr, col_dev(cc))
            return carry

        lax.fori_loop(1, N_COL, to_col, 0)

        def to_hid(d, carry):
            kk = (h + d) % N_HID
            send(k_slice(kk), rk.at[own_slot], ks, kr, (kk, c))
            return carry

        lax.fori_loop(1, N_HID, to_hid, 0)

    up, down = (y + 1) % NY, (y + NY - 1) % NY

    def y_block(hop, way, j):
        yy = (y - hop + NY) % NY if way == 0 else (y + hop) % NY
        return rn.at[slot_of(yy, (z + j) % NZ)]

    def y_hops(way, j):
        return 4 if (j < 2) == (way == 0) else 3

    def y_send(hop, way, j):
        block = y_block(hop, way, j)
        send(block, block, yas, yar.at[way, hop, j], hid_dev(up if way == 0 else down, z))

    wait_for(rn.at[own_slot], nr)
    for way in range(2):
        y_send(0, way, 0)
    for d in range(1, NZ):
        send(rn.at[own_slot], rn.at[own_slot], zas, zar.at[NZ - d], hid_dev(y, (z + d) % NZ))
    wait_for(rk.at[pl.ds(k_base, 2)], kr)
    k_two = rk.at[pl.ds(k_base, 2)]
    send(k_two, k_two, khs, khr, col_dev(zh_c))
    for j in range(1, NZ):
        wait_for(rn.at[slot_of(y, (z + j) % NZ)], zar.at[j])
        for way in range(2):
            y_send(0, way, j)
    k_four = rk.at[pl.ds(core * 16 + x * 4, 4)]
    for hop in range(1, 5):
        for j in range(NZ):
            for way in range(2):
                if hop <= y_hops(way, j):
                    wait_for(y_block(hop, way, j), yar.at[way, hop - 1, j])
                    if hop < y_hops(way, j):
                        y_send(hop, way, j)
        if hop == 1:
            wait_for(rk.at[pl.ds(core * 16 + x * 4 + (1 - zh) * 2, 2)], khr)
            for d in range(1, 4):
                xx = (x + d) % 4
                send(k_four, k_four, kxs, kxr.at[d - 1], col_dev((xx * 2 + zh) * 2 + core))
        if hop == 3:
            for d in range(1, 4):
                wait_for(rk.at[pl.ds(core * 16 + ((x + 4 - d) % 4) * 4, 4)], kxr.at[d - 1])
            k_all = rk.at[pl.ds(core * 16, 16)]
            send(k_all, k_all, kcs, kcr, col_dev(m * 2 + 1 - core))
    wait_for(rk.at[pl.ds((1 - core) * 16, 16)], kcr)

    off = 64 * (h % 2)
    rkt[...] = rk[...].reshape(512, KP).T
    loads[4].wait()
    factor = gram_weight / EXAMPLES
    for b in range(3):
        left = rkt[pl.ds(pl.multiple_of(off + 192 * b, 64), 192), :]
        for n in range(3):
            cols = slice(384 * n, 384 * (n + 1))
            gram = jnp.dot(left, rn[:, :, cols].reshape(512, 384), preferred_element_type=F32)
            new = cv[192 * b : 192 * (b + 1), cols].astype(F32) + gram * factor
            cn[pl.ds(pl.multiple_of(off + 192 * b, 64), 192), cols] = new.astype(BF16)
    out = pltpu.make_async_copy(cn.at[pl.ds(pl.multiple_of(off, 64), KW)], cn_hbm, out_sem)
    out.start()

    for b in range(4):
        prod = jnp.dot(
            rk[8 * b : 8 * (b + 1)].reshape(128, KP), cn[...], preferred_element_type=F32
        )
        p[8 * b : 8 * (b + 1)] = (prod * apply_weight).astype(BF16).reshape(8, 16, NW)

    def p_slot(left_hops, way, j):
        yy = (y + left_hops) % NY if way == 0 else (y - left_hops + NY) % NY
        return slot_of(yy, j)

    for step in range(4):
        for j in range(NZ):
            for way in range(2):
                hops = y_hops(way, j)
                left = 4 - step
                if left > hops:
                    continue
                at = p_slot(left, way, j)
                if left == hops:
                    src = p.at[at]
                else:
                    src = rp.at[way, step - 1, j]
                    wait_for(src, rpr.at[way, step - 1, j])
                    src[...] = (src[...].astype(F32) + p[at].astype(F32)).astype(BF16)
                send(src, rp.at[way, step, j], rps, rpr.at[way, step, j],
                     hid_dev(up if way == 0 else down, z))
    for j in range(NZ):
        for way in range(2):
            wait_for(rp.at[way, 3, j], rpr.at[way, 3, j])
        done = p[slot_of(y, j)].astype(F32)
        for way in range(2):
            done = done + rp[way, 3, j].astype(F32)
        zs[j] = done.astype(BF16)

        @pl.when(z != j)
        def _():
            send(zs.at[j], zr.at[(j - z + NZ) % NZ - 1], zrs, zrr, hid_dev(y, j))

    wait_for(zr, zrr)
    final = zs[z].astype(F32)
    for d in range(3):
        final = final + zr[d].astype(F32)
    app_ref[...] = final[0:OWN, :]

    wait_for(r1, a1s)
    wait_for(rn.at[pl.ds(0, 3)], zas)
    wait_for(rn.at[pl.ds(0, 28)], yas)
    wait_for(rk.at[pl.ds(0, 2)], khs)
    wait_for(rk.at[pl.ds(0, 12)], kxs)
    wait_for(rk.at[pl.ds(0, 16)], kcs)
    wait_for(rn.at[pl.ds(0, 28)], rps)
    wait_for(zr, zrs)

    @pl.when(is_root)
    def _():
        wait_for(rn.at[pl.ds(0, 15)], ns)
        wait_for(rk.at[pl.ds(0, 31)], ks)

    out.wait()


def per_device(inputs, out_grads, proj_in, proj_out, curvature):
    dma = pltpu.SemaphoreType.DMA
    vm = pltpu.VMEM
    hbm = pl.BlockSpec(memory_space=pl.ANY)
    return pl.pallas_call(
        kernel,
        out_shape=(
            jax.ShapeDtypeStruct((OWN, NW), F32),
            jax.ShapeDtypeStruct((KW, NW), BF16),
        ),
        in_specs=[hbm] * 5,
        out_specs=(pl.BlockSpec(memory_space=pltpu.VMEM), hbm),
        scratch_shapes=[
            vm(inputs.shape, BF16), vm(out_grads.shape, BF16), vm(proj_in.shape, BF16),
            vm(proj_out.shape, BF16), vm(curvature.shape, BF16),
            vm((8, FEATS, 128), BF16), vm((7, FEATS, 128), BF16), vm((FEATS, 128), BF16),
            vm((3, FEATS, 128), BF16), vm((FEATS, 128), BF16), vm((FEATS, 512), BF16),
            vm((PIN, 512), F32), vm((256, 512), BF16), vm((256, 512), BF16),
            vm((16, PIN * POUT), BF16),
            vm((32, 16, NW), BF16), vm((32, 16, KP), BF16), vm((KP, 512), BF16),
            vm((KP, NW), BF16), vm((32, 16, NW), BF16), vm((2, 4, 4, 16, NW), BF16),
            vm((4, 16, NW), BF16), vm((3, 16, NW), BF16),
            dma((5,)), dma, dma, dma, dma, dma, dma, dma, dma, dma, dma,
            dma, dma((4,)), dma, dma((2, 4, 4)), dma, dma, dma, dma((3,)), dma, dma,
            dma, dma((2, 4, 4)), dma, dma, dma,
        ],
        compiler_params=pltpu.CompilerParams(
            collective_id=0, has_side_effects=True, vmem_limit_bytes=48 * 2**20
        ),
    )(inputs, out_grads, proj_in, proj_out, curvature)


def solution(mesh):
    in_specs = (P("col", "hid"), P("col", "hid"), P(None, "hid"), P(None, "hid"), P("hid", "col"))
    out_specs = (P("hid", "col"), P("hid", "col"))
    return jax.shard_map(
        per_device, mesh=mesh, in_specs=in_specs, out_specs=out_specs, check_vma=False
    )
```

```python
import jax
import jax.numpy as jnp
from jax import lax
from jax.experimental import pallas as pl
from jax.experimental.pallas import tpu as pltpu
from jax.sharding import PartitionSpec as P

MESH = pl.DeviceIdType.MESH
F32 = jnp.float32
BF16 = jnp.bfloat16

PIN = 96
POUT = 192
FEATS = PIN + POUT
SEQ = 32
EXAMPLES = 480
NY, NZ = 8, 4
N_HID, N_COL = 32, 16
OWN = 15
TOK = OWN * SEQ
NW = 1152
KW = 576
KP = 640
gram_weight = 1.0 / 64.0
apply_weight = 1.0 / 16.0
NT = (((1,), (1,)), ((), ()))


def slot_of(y, z):
    return (z // 2) * 16 + y * 2 + z % 2


def root_group(y, z):
    return (y + 16 - 4 * (z % 2) - 2 * (z // 2)) % NY


def block_slot(y, z):
    return slot_of(root_group(y, z), z)


def kernel(
    x_hbm, g_hbm, wi_hbm, wo_hbm, c_hbm,
    app_ref, cn_hbm,
    xv, gv, wiv, wov, cv,
    part, r1, s1, r2, s2, r3, featv, ge, go, rows,
    rn, rk, rkt, cn, p, rp, zs, zr,
    in_sem, a1s, a1r, a2s, a2r, a3s, a3r, ns, nr, ks, kr,
    zas, zar, yas, yar, khs, khr, kxs, kxr, kcs, kcr,
    rps, rpr, zrs, zrr, out_sem,
):
    h = lax.axis_index("hid")
    c = lax.axis_index("col")
    y, z = h // NZ, h % NZ
    core = c % 2
    m = c // 2
    x, zh = m // 2, m % 2
    first_y = (m + 2 * core + NY - 1) % NY

    def chunk_of(yy):
        return (yy + NY - first_y) % NY

    z_target = 2 * core + chunk_of(y) // 4
    y_root = (m + 4 * (z % 2) + 2 * (z // 2)) % NY
    is_target = z == z_target
    is_root = jnp.logical_and(y == y_root, core == z // 2)
    own_slot = block_slot(y, z)

    def hid_dev(yy, zz):
        return (yy * NZ + zz, c)

    def col_dev(cc):
        return (h, cc)

    def send(src, dst, ssem, rsem, dev):
        copy = pltpu.make_async_remote_copy(
            src_ref=src, dst_ref=dst, send_sem=ssem, recv_sem=rsem,
            device_id=dev, device_id_type=MESH,
        )
        copy.start()

    def wait_for(ref, sem):
        pltpu.make_async_copy(ref, ref, sem).wait()

    loads = []
    for i, (src, dst) in enumerate(
        ((x_hbm, xv), (wi_hbm, wiv), (g_hbm, gv), (wo_hbm, wov), (c_hbm, cv))
    ):
        load = pltpu.make_async_copy(src, dst, in_sem.at[i])
        load.start()
        loads.append(load)

    barrier = pltpu.get_barrier_semaphore()

    def greet(dev):
        pl.semaphore_signal(barrier, inc=1, device_id=dev, device_id_type=MESH)

    for d in range(1, NY):
        greet(hid_dev((y + d) % NY, z))
    for d in range(1, NZ):
        greet(hid_dev(y, (z + d) % NZ))
    zh_c = (x * 2 + (1 - zh)) * 2 + core
    greet(col_dev(zh_c))
    for d in range(1, 4):
        greet(col_dev((((x + d) % 4) * 2 + zh) * 2 + core))
    greet(col_dev(m * 2 + 1 - core))

    @pl.when(jnp.logical_not(is_root))
    def _():
        greet(col_dev(root_group(y, z) * 2 + z // 2))

    zero_tail = jnp.zeros((FEATS, 128), BF16)
    for hf in range(2):
        part[4 * hf + 3] = zero_tail
    loads[2].wait()
    loads[3].wait()

    def project(w, v, first):
        for hf in range(2):
            t = lax.dot_general(
                w[...], v[TOK * hf : TOK * (hf + 1), :], NT, preferred_element_type=F32
            ).astype(BF16)
            n = t.shape[0]
            for q in range(3):
                part[4 * hf + q, first : first + n, :] = t[:, 128 * q : 128 * (q + 1)]
            part[4 * hf + 3, first : first + n, 0:96] = t[:, 384:480]

    project(wov, gv, 0)
    loads[0].wait()
    loads[1].wait()
    project(wiv, xv, POUT)

    pl.semaphore_wait(barrier, jnp.where(is_root, 30, 15))

    for d in (4, 3, 5, 2, 6, 1, 7):
        yy = (y + d) % NY
        send(part.at[chunk_of(yy)], r1.at[d - 1], a1s, a1r, hid_dev(yy, z))
    parity_zero = jnp.zeros((64, NW), BF16)
    cn[pl.ds(pl.multiple_of(KW * (1 - h % 2), 64), 64), :] = parity_zero
    wait_for(r1, a1r)
    total = part[chunk_of(y)].astype(F32)
    for d in range(7):
        total = total + r1[d].astype(F32)
    s1[...] = total.astype(BF16)


    @pl.when(jnp.logical_not(is_target))
    def _():
        send(s1, r2.at[(z - z_target + NZ) % NZ - 1], a2s, a2r, hid_dev(y, z_target))
        wait_for(s1, a2s)

    @pl.when(is_target)
    def _():
        wait_for(r2, a2r)
        whole = s1[...].astype(F32)
        for d in range(3):
            whole = whole + r2[d].astype(F32)
        s2[...] = whole.astype(BF16)
        place = r3.at[:, pl.ds(pl.multiple_of(128 * (chunk_of(y) % 4), 128), 128)]

        @pl.when(y != y_root)
        def _():
            send(s2, place, a3s, a3r, hid_dev(y_root, z))
            wait_for(s2, a3s)

        @pl.when(y == y_root)
        def _():
            pltpu.make_async_copy(s2, place, a3r).start()

    k_base = core * 16 + m * 2

    @pl.when(is_root)
    def _():
        wait_for(r3, a3r)
        ge[0:POUT, :] = r3[0:POUT, :]
        ge[POUT:256, :] = jnp.zeros((64, 512), BF16)
        go[0:64, :] = jnp.zeros((64, 512), BF16)
        go[64:256, :] = r3[0:POUT, :]
        featv[...] = r3[POUT:FEATS, :].astype(F32)
        mine = (
            lax.broadcasted_iota(jnp.int32, (16, 512), 1) // SEQ
            == lax.broadcasted_iota(jnp.int32, (16, 512), 0)
        )

        def form(i, carry):
            def spread(odd):
                return jnp.concatenate(
                    [
                        jnp.where(
                            mine,
                            jnp.broadcast_to(featv[pl.ds(i * 24 + 2 * q + odd, 1), :], (16, 512)),
                            0.0,
                        ).astype(BF16)
                        for q in range(12)
                    ],
                    axis=0,
                )

            even = lax.dot_general(spread(0), ge[...], NT, preferred_element_type=F32)
            odd = lax.dot_general(spread(1), go[...], NT, preferred_element_type=F32)
            for q in range(12):
                e = even[16 * q : 16 * (q + 1)]
                o = odd[16 * q : 16 * (q + 1)]
                three = jnp.concatenate(
                    [e[:, 0:128], e[:, 128:256] + o[:, 0:128], o[:, 128:256]], axis=1
                )
                at = pl.multiple_of(i * 4608 + 384 * q, 128)
                rows[:, pl.ds(at, 384)] = three.astype(BF16)
            return carry

        lax.fori_loop(0, 4, form, 0)

        def n_slice(cc):
            return rows.at[:, pl.ds(pl.multiple_of(cc * NW, 128), NW)]

        def k_slice(kk):
            return rows.at[:, pl.ds(pl.multiple_of((kk // 2) * NW + (kk % 2) * 512, 128), KP)]

        pltpu.make_async_copy(n_slice(c), rn.at[own_slot], nr).start()
        pltpu.make_async_copy(k_slice(h), rk.at[own_slot], kr).start()

        def to_col(d, carry):
            cc = (c + d) % N_COL
            send(n_slice(cc), rn.at[own_slot], ns, nr, col_dev(cc))
            return carry

        lax.fori_loop(1, N_COL, to_col, 0)

        def to_hid(d, carry):
            kk = (h + d) % N_HID
            send(k_slice(kk), rk.at[own_slot], ks, kr, (kk, c))
            return carry

        lax.fori_loop(1, N_HID, to_hid, 0)

    up, down = (y + 1) % NY, (y + NY - 1) % NY

    def y_block(hop, way, j):
        yy = (y - hop + NY) % NY if way == 0 else (y + hop) % NY
        return rn.at[block_slot(yy, (z + j) % NZ)]

    def y_hops(way, j):
        return 4 if (j < 2) == (way == 0) else 3

    def y_send(hop, way, j):
        block = y_block(hop, way, j)
        send(block, block, yas, yar.at[way, hop, j], hid_dev(up if way == 0 else down, z))

    wait_for(rn.at[own_slot], nr)
    for way in range(2):
        y_send(0, way, 0)
    for d in range(1, NZ):
        send(rn.at[own_slot], rn.at[own_slot], zas, zar.at[NZ - d], hid_dev(y, (z + d) % NZ))
    wait_for(rk.at[pl.ds(k_base, 2)], kr)
    k_two = rk.at[pl.ds(k_base, 2)]
    send(k_two, k_two, khs, khr, col_dev(zh_c))
    for j in range(1, NZ):
        wait_for(rn.at[block_slot(y, (z + j) % NZ)], zar.at[j])
        for way in range(2):
            y_send(0, way, j)
    k_four = rk.at[pl.ds(core * 16 + x * 4, 4)]
    for hop in range(1, 5):
        for j in range(NZ):
            for way in range(2):
                if hop <= y_hops(way, j):
                    wait_for(y_block(hop, way, j), yar.at[way, hop - 1, j])
                    if hop < y_hops(way, j):
                        y_send(hop, way, j)
        if hop == 1:
            wait_for(rk.at[pl.ds(core * 16 + x * 4 + (1 - zh) * 2, 2)], khr)
            for d in range(1, 4):
                xx = (x + d) % 4
                send(k_four, k_four, kxs, kxr.at[d - 1], col_dev((xx * 2 + zh) * 2 + core))
        if hop == 3:
            for d in range(1, 4):
                wait_for(rk.at[pl.ds(core * 16 + ((x + 4 - d) % 4) * 4, 4)], kxr.at[d - 1])
            k_all = rk.at[pl.ds(core * 16, 16)]
            send(k_all, k_all, kcs, kcr, col_dev(m * 2 + 1 - core))
    wait_for(rk.at[pl.ds((1 - core) * 16, 16)], kcr)

    off = 64 * (h % 2)
    rkt[...] = rk[...].reshape(512, KP).T
    loads[4].wait()
    factor = gram_weight / EXAMPLES
    for b in range(3):
        left = rkt[pl.ds(pl.multiple_of(off + 192 * b, 64), 192), :]
        for n in range(3):
            cols = slice(384 * n, 384 * (n + 1))
            gram = jnp.dot(left, rn[:, :, cols].reshape(512, 384), preferred_element_type=F32)
            new = cv[192 * b : 192 * (b + 1), cols].astype(F32) + gram * factor
            cn[pl.ds(pl.multiple_of(off + 192 * b, 64), 192), cols] = new.astype(BF16)
    out = pltpu.make_async_copy(cn.at[pl.ds(pl.multiple_of(off, 64), KW)], cn_hbm, out_sem)
    out.start()

    for b in range(4):
        prod = jnp.dot(
            rk[8 * b : 8 * (b + 1)].reshape(128, KP), cn[...], preferred_element_type=F32
        )
        p[8 * b : 8 * (b + 1)] = (prod * apply_weight).astype(BF16).reshape(8, 16, NW)

    def p_slot(left_hops, way, j):
        yy = (y + left_hops) % NY if way == 0 else (y - left_hops + NY) % NY
        return slot_of(yy, j)

    for step in range(4):
        for j in range(NZ):
            for way in range(2):
                hops = y_hops(way, j)
                left = 4 - step
                if left > hops:
                    continue
                at = p_slot(left, way, j)
                if left == hops:
                    src = p.at[at]
                else:
                    src = rp.at[way, step - 1, j]
                    wait_for(src, rpr.at[way, step - 1, j])
                    src[...] = (src[...].astype(F32) + p[at].astype(F32)).astype(BF16)
                send(src, rp.at[way, step, j], rps, rpr.at[way, step, j],
                     hid_dev(up if way == 0 else down, z))
    for j in range(NZ):
        for way in range(2):
            wait_for(rp.at[way, 3, j], rpr.at[way, 3, j])
        done = p[slot_of(y, j)].astype(F32)
        for way in range(2):
            done = done + rp[way, 3, j].astype(F32)
        zs[j] = done.astype(BF16)

        @pl.when(z != j)
        def _():
            send(zs.at[j], zr.at[(j - z + NZ) % NZ - 1], zrs, zrr, hid_dev(y, j))

    wait_for(zr, zrr)
    final = zs[z].astype(F32)
    for d in range(3):
        final = final + zr[d].astype(F32)
    app_ref[...] = final[0:OWN, :]

    wait_for(r1, a1s)
    wait_for(rn.at[pl.ds(0, 3)], zas)
    wait_for(rn.at[pl.ds(0, 28)], yas)
    wait_for(rk.at[pl.ds(0, 2)], khs)
    wait_for(rk.at[pl.ds(0, 12)], kxs)
    wait_for(rk.at[pl.ds(0, 16)], kcs)
    wait_for(rn.at[pl.ds(0, 28)], rps)
    wait_for(zr, zrs)

    @pl.when(is_root)
    def _():
        wait_for(rn.at[pl.ds(0, 15)], ns)
        wait_for(rk.at[pl.ds(0, 31)], ks)

    out.wait()


def per_device(inputs, out_grads, proj_in, proj_out, curvature):
    dma = pltpu.SemaphoreType.DMA
    vm = pltpu.VMEM
    hbm = pl.BlockSpec(memory_space=pl.ANY)
    return pl.pallas_call(
        kernel,
        out_shape=(
            jax.ShapeDtypeStruct((OWN, NW), F32),
            jax.ShapeDtypeStruct((KW, NW), BF16),
        ),
        in_specs=[hbm] * 5,
        out_specs=(pl.BlockSpec(memory_space=pltpu.VMEM), hbm),
        scratch_shapes=[
            vm(inputs.shape, BF16), vm(out_grads.shape, BF16), vm(proj_in.shape, BF16),
            vm(proj_out.shape, BF16), vm(curvature.shape, BF16),
            vm((8, FEATS, 128), BF16), vm((7, FEATS, 128), BF16), vm((FEATS, 128), BF16),
            vm((3, FEATS, 128), BF16), vm((FEATS, 128), BF16), vm((FEATS, 512), BF16),
            vm((PIN, 512), F32), vm((256, 512), BF16), vm((256, 512), BF16),
            vm((16, PIN * POUT), BF16),
            vm((32, 16, NW), BF16), vm((32, 16, KP), BF16), vm((KP, 512), BF16),
            vm((KP, NW), BF16), vm((32, 16, NW), BF16), vm((2, 4, 4, 16, NW), BF16),
            vm((4, 16, NW), BF16), vm((3, 16, NW), BF16),
            dma((5,)), dma, dma, dma, dma, dma, dma, dma, dma, dma, dma,
            dma, dma((4,)), dma, dma((2, 4, 4)), dma, dma, dma, dma((3,)), dma, dma,
            dma, dma((2, 4, 4)), dma, dma, dma,
        ],
        compiler_params=pltpu.CompilerParams(
            collective_id=0, has_side_effects=True, vmem_limit_bytes=60 * 2**20
        ),
    )(inputs, out_grads, proj_in, proj_out, curvature)


def solution(mesh):
    in_specs = (P("col", "hid"), P("col", "hid"), P(None, "hid"), P(None, "hid"), P("hid", "col"))
    out_specs = (P("hid", "col"), P("hid", "col"))
    return jax.shard_map(
        per_device, mesh=mesh, in_specs=in_specs, out_specs=out_specs, check_vma=False
    )
```

```python
import jax
import jax.numpy as jnp
from jax import lax
from jax.experimental import pallas as pl
from jax.experimental.pallas import tpu as pltpu
from jax.sharding import PartitionSpec as P

MESH = pl.DeviceIdType.MESH
F32 = jnp.float32
BF16 = jnp.bfloat16

PIN = 96
POUT = 192
FEATS = PIN + POUT
SEQ = 32
EXAMPLES = 480
NY, NZ = 8, 4
N_HID, N_COL = 32, 16
OWN = 15
TOK = OWN * SEQ
NW = 1152
KW = 576
KP = 640
gram_weight = 1.0 / 64.0
apply_weight = 1.0 / 16.0
NT = (((1,), (1,)), ((), ()))


def slot_of(y, z):
    return (z // 2) * 16 + y * 2 + z % 2


def root_group(y, z):
    return (y + 16 - 4 * (z % 2) - 2 * (z // 2)) % NY


def block_slot(y, z):
    return slot_of(root_group(y, z), z)


def kernel(
    x_hbm, g_hbm, wi_hbm, wo_hbm, c_hbm,
    app_ref, cn_hbm,
    xv, gv, wiv, wov, cx,
    part, r1, s1, r2, s2, r3, featv, ge, go, rows,
    rn, rk, rkt, cn, p, rp, zs, zr, sp, sq, sr, sall,
    in_sem, a1s, a1r, a2s, a2r, a3s, a3r, ns, nr, ks, kr,
    zas, zar, yas, yar, khs, khr, kxs, kxr, kcs, kcr,
    rps, rpr, zrs, zrr, scs, scr, sms, smr, out_sem,
):
    h = lax.axis_index("hid")
    c = lax.axis_index("col")
    y, z = h // NZ, h % NZ
    core = c % 2
    m = c // 2
    x, zh = m // 2, m % 2
    first_y = (m + 2 * core + NY - 1) % NY

    def chunk_of(yy):
        return (yy + NY - first_y) % NY

    z_target = 2 * core + chunk_of(y) // 4
    y_root = (m + 4 * (z % 2) + 2 * (z // 2)) % NY
    is_target = z == z_target
    is_root = jnp.logical_and(y == y_root, core == z // 2)
    own_slot = block_slot(y, z)

    def hid_dev(yy, zz):
        return (yy * NZ + zz, c)

    def col_dev(cc):
        return (h, cc)

    def send(src, dst, ssem, rsem, dev):
        copy = pltpu.make_async_remote_copy(
            src_ref=src, dst_ref=dst, send_sem=ssem, recv_sem=rsem,
            device_id=dev, device_id_type=MESH,
        )
        copy.start()

    def wait_for(ref, sem):
        pltpu.make_async_copy(ref, ref, sem).wait()

    off = pl.multiple_of(64 * (h % 2), 64)
    loads = []
    for i, (src, dst) in enumerate(
        (
            (x_hbm, xv), (wi_hbm, wiv), (g_hbm, gv), (wo_hbm, wov),
            (c_hbm, cx.at[pl.ds(off, KW)]),
        )
    ):
        load = pltpu.make_async_copy(src, dst, in_sem.at[i])
        load.start()
        loads.append(load)

    barrier = pltpu.get_barrier_semaphore()

    def greet(dev):
        pl.semaphore_signal(barrier, inc=1, device_id=dev, device_id_type=MESH)

    for d in range(1, NY):
        greet(hid_dev((y + d) % NY, z))
    for d in range(1, NZ):
        greet(hid_dev(y, (z + d) % NZ))
    zh_c = (x * 2 + (1 - zh)) * 2 + core
    greet(col_dev(zh_c))
    for d in range(1, 4):
        greet(col_dev((((x + d) % 4) * 2 + zh) * 2 + core))
    greet(col_dev(m * 2 + 1 - core))

    @pl.when(jnp.logical_not(is_root))
    def _():
        greet(col_dev(root_group(y, z) * 2 + z // 2))

    zero_tail = jnp.zeros((FEATS, 128), BF16)
    for hf in range(2):
        part[4 * hf + 3] = zero_tail
    loads[2].wait()
    loads[3].wait()

    def project(w, v, first):
        for hf in range(2):
            t = lax.dot_general(
                w[...], v[TOK * hf : TOK * (hf + 1), :], NT, preferred_element_type=F32
            ).astype(BF16)
            n = t.shape[0]
            for q in range(3):
                part[4 * hf + q, first : first + n, :] = t[:, 128 * q : 128 * (q + 1)]
            part[4 * hf + 3, first : first + n, 0:96] = t[:, 384:480]

    project(wov, gv, 0)
    loads[0].wait()
    loads[1].wait()
    project(wiv, xv, POUT)

    pl.semaphore_wait(barrier, jnp.where(is_root, 30, 15))

    for d in (4, 3, 5, 2, 6, 1, 7):
        yy = (y + d) % NY
        send(part.at[chunk_of(yy)], r1.at[d - 1], a1s, a1r, hid_dev(yy, z))
    cx[pl.ds(pl.multiple_of(KW * (1 - h % 2), 64), 64), :] = jnp.zeros((64, NW), BF16)
    wait_for(r1, a1r)
    total = part[chunk_of(y)].astype(F32)
    for d in range(7):
        total = total + r1[d].astype(F32)
    s1[...] = total.astype(BF16)


    @pl.when(jnp.logical_not(is_target))
    def _():
        send(s1, r2.at[(z - z_target + NZ) % NZ - 1], a2s, a2r, hid_dev(y, z_target))
        wait_for(s1, a2s)

    @pl.when(is_target)
    def _():
        wait_for(r2, a2r)
        whole = s1[...].astype(F32)
        for d in range(3):
            whole = whole + r2[d].astype(F32)
        s2[...] = whole.astype(BF16)
        place = r3.at[:, pl.ds(pl.multiple_of(128 * (chunk_of(y) % 4), 128), 128)]

        @pl.when(y != y_root)
        def _():
            send(s2, place, a3s, a3r, hid_dev(y_root, z))
            wait_for(s2, a3s)

        @pl.when(y == y_root)
        def _():
            pltpu.make_async_copy(s2, place, a3r).start()

    k_base = core * 16 + m * 2

    @pl.when(is_root)
    def _():
        wait_for(r3, a3r)
        ge[0:POUT, :] = r3[0:POUT, :]
        ge[POUT:256, :] = jnp.zeros((64, 512), BF16)
        go[0:64, :] = jnp.zeros((64, 512), BF16)
        go[64:256, :] = r3[0:POUT, :]
        featv[...] = r3[POUT:FEATS, :].astype(F32)
        mine = (
            lax.broadcasted_iota(jnp.int32, (16, 512), 1) // SEQ
            == lax.broadcasted_iota(jnp.int32, (16, 512), 0)
        )

        def form(i, carry):
            def spread(odd):
                return jnp.concatenate(
                    [
                        jnp.where(
                            mine,
                            jnp.broadcast_to(featv[pl.ds(i * 24 + 2 * q + odd, 1), :], (16, 512)),
                            0.0,
                        ).astype(BF16)
                        for q in range(12)
                    ],
                    axis=0,
                )

            even = lax.dot_general(spread(0), ge[...], NT, preferred_element_type=F32)
            odd = lax.dot_general(spread(1), go[...], NT, preferred_element_type=F32)
            for q in range(12):
                e = even[16 * q : 16 * (q + 1)]
                o = odd[16 * q : 16 * (q + 1)]
                three = jnp.concatenate(
                    [e[:, 0:128], e[:, 128:256] + o[:, 0:128], o[:, 128:256]], axis=1
                )
                at = pl.multiple_of(i * 4608 + 384 * q, 128)
                rows[:, pl.ds(at, 384)] = three.astype(BF16)
            return carry

        lax.fori_loop(0, 4, form, 0)

        def n_slice(cc):
            return rows.at[:, pl.ds(pl.multiple_of(cc * NW, 128), NW)]

        def k_slice(kk):
            return rows.at[:, pl.ds(pl.multiple_of((kk // 2) * NW + (kk % 2) * 512, 128), KP)]

        pltpu.make_async_copy(n_slice(c), rn.at[own_slot], nr).start()
        pltpu.make_async_copy(k_slice(h), rk.at[own_slot], kr).start()

        def to_col(d, carry):
            cc = (c + d) % N_COL
            send(n_slice(cc), rn.at[own_slot], ns, nr, col_dev(cc))
            return carry

        lax.fori_loop(1, N_COL, to_col, 0)

        def to_hid(d, carry):
            kk = (h + d) % N_HID
            send(k_slice(kk), rk.at[own_slot], ks, kr, (kk, c))
            return carry

        lax.fori_loop(1, N_HID, to_hid, 0)

    up, down = (y + 1) % NY, (y + NY - 1) % NY

    def y_block(hop, way, j):
        yy = (y - hop + NY) % NY if way == 0 else (y + hop) % NY
        return rn.at[block_slot(yy, (z + j) % NZ)]

    def y_hops(way, j):
        return 4 if (j < 2) == (way == 0) else 3

    def y_send(hop, way, j):
        block = y_block(hop, way, j)
        send(block, block, yas, yar.at[way, hop, j], hid_dev(up if way == 0 else down, z))

    wait_for(rn.at[own_slot], nr)
    for way in range(2):
        y_send(0, way, 0)
    for d in range(1, NZ):
        send(rn.at[own_slot], rn.at[own_slot], zas, zar.at[NZ - d], hid_dev(y, (z + d) % NZ))
    wait_for(rk.at[pl.ds(k_base, 2)], kr)
    k_two = rk.at[pl.ds(k_base, 2)]
    send(k_two, k_two, khs, khr, col_dev(zh_c))
    for j in range(1, NZ):
        wait_for(rn.at[block_slot(y, (z + j) % NZ)], zar.at[j])
        for way in range(2):
            y_send(0, way, j)

    def y_round(hop):
        for j in range(NZ):
            for way in range(2):
                if hop <= y_hops(way, j):
                    wait_for(y_block(hop, way, j), yar.at[way, hop - 1, j])
                    if hop < y_hops(way, j):
                        y_send(hop, way, j)

    def p_slot(left_hops, way, j):
        yy = (y + left_hops) % NY if way == 0 else (y - left_hops + NY) % NY
        return slot_of(yy, j)

    def p_round(step):
        for j in range(NZ):
            for way in range(2):
                hops = y_hops(way, j)
                left = 4 - step
                if left > hops:
                    continue
                at = p_slot(left, way, j)
                if left == hops:
                    src = p.at[at]
                else:
                    src = rp.at[way, step - 1, j]
                    wait_for(src, rpr.at[way, step - 1, j])
                    src[...] = (src[...].astype(F32) + p[at].astype(F32)).astype(BF16)
                send(src, rp.at[way, step, j], rps, rpr.at[way, step, j],
                     hid_dev(up if way == 0 else down, z))

    wait_for(rk.at[pl.ds(core * 16 + x * 4 + (1 - zh) * 2, 2)], khr)
    k_four = rk.at[pl.ds(core * 16 + x * 4, 4)]
    for d in range(1, 4):
        xx = (x + d) % 4
        send(k_four, k_four, kxs, kxr.at[d - 1], col_dev((xx * 2 + zh) * 2 + core))
    y_round(1)
    for d in range(1, 4):
        wait_for(rk.at[pl.ds(core * 16 + ((x + 4 - d) % 4) * 4, 4)], kxr.at[d - 1])
    k_all = rk.at[pl.ds(core * 16, 16)]
    send(k_all, k_all, kcs, kcr, col_dev(m * 2 + 1 - core))
    y_round(2)
    wait_for(rk.at[pl.ds((1 - core) * 16, 16)], kcr)
    loads[4].wait()
    for b in range(4):
        prod = jnp.dot(
            rk[8 * b : 8 * (b + 1)].reshape(128, KP), cx[...], preferred_element_type=F32
        )
        p[8 * b : 8 * (b + 1)] = (prod * apply_weight).astype(BF16).reshape(8, 16, NW)
    p_round(0)
    y_round(3)
    p_round(1)
    y_round(4)

    sp[...] = lax.dot_general(
        rn[slot_of(y, z)], rn[...].reshape(512, NW), NT, preferred_element_type=F32
    ).astype(BF16)
    send(sp, sq, scs, scr, col_dev(m * 2 + 1 - core))
    p_round(2)
    wait_for(sq, scr)
    sall[...] = (sp[...].astype(F32) + sq[...].astype(F32)).astype(BF16)
    for d in range(1, 8):
        send(sall, sr.at[d - 1], sms, smr, col_dev(((m + d) % 8) * 2 + core))

    rkt[...] = rk[...].reshape(512, KP).T
    factor = gram_weight / EXAMPLES
    for b in range(3):
        lines = pl.ds(pl.multiple_of(off + 192 * b, 64), 192)
        left = rkt[lines, :]
        for n in range(3):
            cols = slice(384 * n, 384 * (n + 1))
            gram = jnp.dot(left, rn[:, :, cols].reshape(512, 384), preferred_element_type=F32)
            new = cx[lines, cols].astype(F32) + gram * factor
            cn[192 * b : 192 * (b + 1), cols] = new.astype(BF16)
    out = pltpu.make_async_copy(cn, cn_hbm, out_sem)
    out.start()

    p_round(3)
    for j in range(NZ):
        for way in range(2):
            wait_for(rp.at[way, 3, j], rpr.at[way, 3, j])
        done = p[slot_of(y, j)].astype(F32)
        for way in range(2):
            done = done + rp[way, 3, j].astype(F32)
        zs[j] = done.astype(BF16)

        @pl.when(z != j)
        def _():
            send(zs.at[j], zr.at[(j - z + NZ) % NZ - 1], zrs, zrr, hid_dev(y, j))

    wait_for(sr, smr)
    s = sall[...].astype(F32)
    for d in range(7):
        s = s + sr[d].astype(F32)
    high = s.astype(BF16)
    low = (s - high.astype(F32)).astype(BF16)
    both = jnp.dot(
        jnp.concatenate([high, low], axis=0), rn[...].reshape(512, NW),
        preferred_element_type=F32,
    )
    final = (both[0:16] + both[16:32]) * (factor * apply_weight) + zs[z].astype(F32)
    wait_for(zr, zrr)
    for d in range(3):
        final = final + zr[d].astype(F32)
    app_ref[...] = final[0:OWN, :]

    wait_for(r1, a1s)
    wait_for(rn.at[pl.ds(0, 3)], zas)
    wait_for(rn.at[pl.ds(0, 28)], yas)
    wait_for(rk.at[pl.ds(0, 2)], khs)
    wait_for(rk.at[pl.ds(0, 12)], kxs)
    wait_for(rk.at[pl.ds(0, 16)], kcs)
    wait_for(rn.at[pl.ds(0, 28)], rps)
    wait_for(zr, zrs)
    wait_for(sp, scs)
    wait_for(sr, sms)

    @pl.when(is_root)
    def _():
        wait_for(rn.at[pl.ds(0, 15)], ns)
        wait_for(rk.at[pl.ds(0, 31)], ks)

    out.wait()


def per_device(inputs, out_grads, proj_in, proj_out, curvature):
    dma = pltpu.SemaphoreType.DMA
    vm = pltpu.VMEM
    hbm = pl.BlockSpec(memory_space=pl.ANY)
    return pl.pallas_call(
        kernel,
        out_shape=(
            jax.ShapeDtypeStruct((OWN, NW), F32),
            jax.ShapeDtypeStruct((KW, NW), BF16),
        ),
        in_specs=[hbm] * 5,
        out_specs=(pl.BlockSpec(memory_space=pltpu.VMEM), hbm),
        scratch_shapes=[
            vm(inputs.shape, BF16), vm(out_grads.shape, BF16), vm(proj_in.shape, BF16),
            vm(proj_out.shape, BF16), vm((KP, NW), BF16),
            vm((8, FEATS, 128), BF16), vm((7, FEATS, 128), BF16), vm((FEATS, 128), BF16),
            vm((3, FEATS, 128), BF16), vm((FEATS, 128), BF16), vm((FEATS, 512), BF16),
            vm((PIN, 512), F32), vm((256, 512), BF16), vm((256, 512), BF16),
            vm((16, PIN * POUT), BF16),
            vm((32, 16, NW), BF16), vm((32, 16, KP), BF16), vm((KP, 512), BF16),
            vm((KW, NW), BF16), vm((32, 16, NW), BF16), vm((2, 4, 4, 16, NW), BF16),
            vm((4, 16, NW), BF16), vm((3, 16, NW), BF16),
            vm((16, 512), BF16), vm((16, 512), BF16), vm((7, 16, 512), BF16), vm((16, 512), BF16),
            dma((5,)), dma, dma, dma, dma, dma, dma, dma, dma, dma, dma,
            dma, dma((4,)), dma, dma((2, 4, 4)), dma, dma, dma, dma((3,)), dma, dma,
            dma, dma((2, 4, 4)), dma, dma, dma, dma, dma, dma, dma,
        ],
        compiler_params=pltpu.CompilerParams(
            collective_id=0, has_side_effects=True, vmem_limit_bytes=60 * 2**20
        ),
    )(inputs, out_grads, proj_in, proj_out, curvature)


def solution(mesh):
    in_specs = (P("col", "hid"), P("col", "hid"), P(None, "hid"), P(None, "hid"), P("hid", "col"))
    out_specs = (P("hid", "col"), P("hid", "col"))
    return jax.shard_map(
        per_device, mesh=mesh, in_specs=in_specs, out_specs=out_specs, check_vma=False
    )
```

```python
import jax
import jax.numpy as jnp
from jax import lax
from jax.experimental import pallas as pl
from jax.experimental.pallas import tpu as pltpu
from jax.sharding import PartitionSpec as P

MESH = pl.DeviceIdType.MESH
F32 = jnp.float32
BF16 = jnp.bfloat16

PIN = 96
POUT = 192
FEATS = PIN + POUT
ZR = 96
YR = FEATS - ZR
SEQ = 32
EXAMPLES = 480
NY, NZ = 8, 4
N_HID, N_COL = 32, 16
OWN = 15
TOK = OWN * SEQ
NW = 1152
KW = 576
KP = 640
gram_weight = 1.0 / 64.0
apply_weight = 1.0 / 16.0
NT = (((1,), (1,)), ((), ()))


def slot_of(y, z):
    return (z // 2) * 16 + y * 2 + z % 2


def root_group(y, z):
    return (y + 16 - 4 * (z % 2) - 2 * (z // 2)) % NY


def block_slot(y, z):
    return slot_of(root_group(y, z), z)


def kernel(
    x_hbm, g_hbm, wi_hbm, wo_hbm, c_hbm,
    app_ref, cn_hbm,
    xv, gv, wiv, wov, cx,
    part, q1, qs, q2, r1, s1, r2, s2, r3, featv, ge, go, rows,
    rn, rk, rkt, cn, p, rp, zs, zr, sp, sq, sr, sall,
    in_sem, q1s, q1r, q2s, q2r, a1s, a1r, a2s, a2r, a3s, a3r, ns, nr, ks, kr,
    zas, zar, yas, yar, khs, khr, kxs, kxr, kcs, kcr,
    rps, rpr, zrs, zrr, scs, scr, sms, smr, out_sem,
):
    h = lax.axis_index("hid")
    c = lax.axis_index("col")
    y, z = h // NZ, h % NZ
    core = c % 2
    m = c // 2
    x, zh = m // 2, m % 2
    first_y = (m + 2 * core + NY - 1) % NY

    def chunk_of(yy):
        return (yy + NY - first_y) % NY

    z_target = 2 * core + chunk_of(y) // 4
    y_root = (m + 4 * (z % 2) + 2 * (z // 2)) % NY
    is_target = z == z_target
    is_root = jnp.logical_and(y == y_root, core == z // 2)
    own_slot = block_slot(y, z)

    def hid_dev(yy, zz):
        return (yy * NZ + zz, c)

    def col_dev(cc):
        return (h, cc)

    def send(src, dst, ssem, rsem, dev):
        copy = pltpu.make_async_remote_copy(
            src_ref=src, dst_ref=dst, send_sem=ssem, recv_sem=rsem,
            device_id=dev, device_id_type=MESH,
        )
        copy.start()

    def wait_for(ref, sem):
        pltpu.make_async_copy(ref, ref, sem).wait()

    off = pl.multiple_of(64 * (h % 2), 64)
    loads = []
    for i, (src, dst) in enumerate(
        (
            (x_hbm, xv), (wi_hbm, wiv), (g_hbm, gv), (wo_hbm, wov),
            (c_hbm, cx.at[pl.ds(off, KW)]),
        )
    ):
        load = pltpu.make_async_copy(src, dst, in_sem.at[i])
        load.start()
        loads.append(load)

    barrier = pltpu.get_barrier_semaphore()

    def greet(dev):
        pl.semaphore_signal(barrier, inc=1, device_id=dev, device_id_type=MESH)

    for d in range(1, NY):
        greet(hid_dev((y + d) % NY, z))
    for d in range(1, NZ):
        greet(hid_dev(y, (z + d) % NZ))
    zh_c = (x * 2 + (1 - zh)) * 2 + core
    greet(col_dev(zh_c))
    for d in range(1, 4):
        greet(col_dev((((x + d) % 4) * 2 + zh) * 2 + core))
    greet(col_dev(m * 2 + 1 - core))

    @pl.when(jnp.logical_not(is_root))
    def _():
        greet(col_dev(root_group(y, z) * 2 + z // 2))

    zero_tail = jnp.zeros((FEATS, 128), BF16)
    for hf in range(2):
        part[4 * hf + 3] = zero_tail
    loads[2].wait()
    loads[3].wait()

    def project(w, v, first):
        for hf in range(2):
            t = lax.dot_general(
                w[...], v[TOK * hf : TOK * (hf + 1), :], NT, preferred_element_type=F32
            ).astype(BF16)
            n = t.shape[0]
            for q in range(3):
                part[4 * hf + q, first : first + n, :] = t[:, 128 * q : 128 * (q + 1)]
            part[4 * hf + 3, first : first + n, 0:96] = t[:, 384:480]

    project(wov, gv, 0)
    loads[0].wait()
    loads[1].wait()
    project(wiv, xv, POUT)

    pl.semaphore_wait(barrier, jnp.where(is_root, 30, 15))

    z_first = pl.ds(0, ZR)
    y_first = pl.ds(ZR, YR)
    for d in (2, 1, 3):
        zz = (z + d) % NZ
        send(part.at[pl.ds(2 * zz, 2), z_first], q1.at[d - 1], q1s, q1r, hid_dev(y, zz))
    for d in (4, 3, 5, 2, 6, 1, 7):
        yy = (y + d) % NY
        send(part.at[chunk_of(yy), y_first], r1.at[d - 1], a1s, a1r, hid_dev(yy, z))
    cx[pl.ds(pl.multiple_of(KW * (1 - h % 2), 64), 64), :] = jnp.zeros((64, NW), BF16)

    wait_for(q1, q1r)
    both = part[pl.ds(2 * z, 2), 0:ZR].astype(F32)
    for d in range(3):
        both = both + q1[d].astype(F32)
    qs[...] = both.astype(BF16)
    q_z = 2 * core + z // 2
    q_y = (m + 4 * (z // 2) + 2 * core) % NY
    q_place = q2.at[y, pl.ds(2 * (z % 2), 2)]
    q_here = jnp.logical_and(q_y == y, q_z == z)

    @pl.when(q_here)
    def _():
        pltpu.make_async_copy(qs, q_place, q2r).start()

    @pl.when(jnp.logical_not(q_here))
    def _():
        send(qs, q_place, q2s, q2r, hid_dev(q_y, q_z))

    wait_for(r1, a1r)
    total = part[chunk_of(y), ZR:FEATS].astype(F32)
    for d in range(7):
        total = total + r1[d].astype(F32)
    s1[...] = total.astype(BF16)

    @pl.when(jnp.logical_not(is_target))
    def _():
        send(s1, r2.at[(z - z_target + NZ) % NZ - 1], a2s, a2r, hid_dev(y, z_target))
        wait_for(s1, a2s)

    @pl.when(is_target)
    def _():
        wait_for(r2, a2r)
        whole = s1[...].astype(F32)
        for d in range(3):
            whole = whole + r2[d].astype(F32)
        s2[...] = whole.astype(BF16)
        place = r3.at[y_first, pl.ds(pl.multiple_of(128 * (chunk_of(y) % 4), 128), 128)]

        @pl.when(y != y_root)
        def _():
            send(s2, place, a3s, a3r, hid_dev(y_root, z))
            wait_for(s2, a3s)

        @pl.when(y == y_root)
        def _():
            pltpu.make_async_copy(s2, place, a3r).start()

    @pl.when(jnp.logical_not(q_here))
    def _():
        wait_for(qs, q2s)

    k_base = core * 16 + m * 2

    @pl.when(is_root)
    def _():
        wait_for(q2, q2r)
        for t in range(4):
            summed = q2[0, t].astype(F32)
            for d in range(1, NY):
                summed = summed + q2[d, t].astype(F32)
            r3[0:ZR, 128 * t : 128 * (t + 1)] = summed.astype(BF16)
        wait_for(r3.at[y_first], a3r)
        ge[0:POUT, :] = r3[0:POUT, :]
        ge[POUT:256, :] = jnp.zeros((64, 512), BF16)
        go[0:64, :] = jnp.zeros((64, 512), BF16)
        go[64:256, :] = r3[0:POUT, :]
        featv[...] = r3[POUT:FEATS, :].astype(F32)
        mine = (
            lax.broadcasted_iota(jnp.int32, (16, 512), 1) // SEQ
            == lax.broadcasted_iota(jnp.int32, (16, 512), 0)
        )

        def form(i, carry):
            def spread(odd):
                return jnp.concatenate(
                    [
                        jnp.where(
                            mine,
                            jnp.broadcast_to(featv[pl.ds(i * 24 + 2 * q + odd, 1), :], (16, 512)),
                            0.0,
                        ).astype(BF16)
                        for q in range(12)
                    ],
                    axis=0,
                )

            even = lax.dot_general(spread(0), ge[...], NT, preferred_element_type=F32)
            odd = lax.dot_general(spread(1), go[...], NT, preferred_element_type=F32)
            for q in range(12):
                e = even[16 * q : 16 * (q + 1)]
                o = odd[16 * q : 16 * (q + 1)]
                three = jnp.concatenate(
                    [e[:, 0:128], e[:, 128:256] + o[:, 0:128], o[:, 128:256]], axis=1
                )
                at = pl.multiple_of(i * 4608 + 384 * q, 128)
                rows[:, pl.ds(at, 384)] = three.astype(BF16)
            return carry

        lax.fori_loop(0, 4, form, 0)

        def n_slice(cc):
            return rows.at[:, pl.ds(pl.multiple_of(cc * NW, 128), NW)]

        def k_slice(kk):
            return rows.at[:, pl.ds(pl.multiple_of((kk // 2) * NW + (kk % 2) * 512, 128), KP)]

        pltpu.make_async_copy(n_slice(c), rn.at[own_slot], nr).start()
        pltpu.make_async_copy(k_slice(h), rk.at[own_slot], kr).start()

        def to_col(d, carry):
            cc = (c + d) % N_COL
            send(n_slice(cc), rn.at[own_slot], ns, nr, col_dev(cc))
            return carry

        lax.fori_loop(1, N_COL, to_col, 0)

        def to_hid(d, carry):
            kk = (h + d) % N_HID
            send(k_slice(kk), rk.at[own_slot], ks, kr, (kk, c))
            return carry

        lax.fori_loop(1, N_HID, to_hid, 0)

    up, down = (y + 1) % NY, (y + NY - 1) % NY

    def y_block(hop, way, j):
        yy = (y - hop + NY) % NY if way == 0 else (y + hop) % NY
        return rn.at[block_slot(yy, (z + j) % NZ)]

    def y_hops(way, j):
        return 4 if (j < 2) == (way == 0) else 3

    def y_send(hop, way, j):
        block = y_block(hop, way, j)
        send(block, block, yas, yar.at[way, hop, j], hid_dev(up if way == 0 else down, z))

    wait_for(rn.at[own_slot], nr)
    for way in range(2):
        y_send(0, way, 0)
    for d in range(1, NZ):
        send(rn.at[own_slot], rn.at[own_slot], zas, zar.at[NZ - d], hid_dev(y, (z + d) % NZ))
    wait_for(rk.at[pl.ds(k_base, 2)], kr)
    k_two = rk.at[pl.ds(k_base, 2)]
    send(k_two, k_two, khs, khr, col_dev(zh_c))
    for j in range(1, NZ):
        wait_for(rn.at[block_slot(y, (z + j) % NZ)], zar.at[j])
        for way in range(2):
            y_send(0, way, j)

    def y_round(hop):
        for j in range(NZ):
            for way in range(2):
                if hop <= y_hops(way, j):
                    wait_for(y_block(hop, way, j), yar.at[way, hop - 1, j])
                    if hop < y_hops(way, j):
                        y_send(hop, way, j)

    def p_slot(left_hops, way, j):
        yy = (y + left_hops) % NY if way == 0 else (y - left_hops + NY) % NY
        return slot_of(yy, j)

    def p_round(step):
        for j in range(NZ):
            for way in range(2):
                hops = y_hops(way, j)
                left = 4 - step
                if left > hops:
                    continue
                at = p_slot(left, way, j)
                if left == hops:
                    src = p.at[at]
                else:
                    src = rp.at[way, step - 1, j]
                    wait_for(src, rpr.at[way, step - 1, j])
                    src[...] = (src[...].astype(F32) + p[at].astype(F32)).astype(BF16)
                send(src, rp.at[way, step, j], rps, rpr.at[way, step, j],
                     hid_dev(up if way == 0 else down, z))

    wait_for(rk.at[pl.ds(core * 16 + x * 4 + (1 - zh) * 2, 2)], khr)
    k_four = rk.at[pl.ds(core * 16 + x * 4, 4)]
    for d in range(1, 4):
        xx = (x + d) % 4
        send(k_four, k_four, kxs, kxr.at[d - 1], col_dev((xx * 2 + zh) * 2 + core))
    y_round(1)
    for d in range(1, 4):
        wait_for(rk.at[pl.ds(core * 16 + ((x + 4 - d) % 4) * 4, 4)], kxr.at[d - 1])
    k_all = rk.at[pl.ds(core * 16, 16)]
    send(k_all, k_all, kcs, kcr, col_dev(m * 2 + 1 - core))
    y_round(2)
    wait_for(rk.at[pl.ds((1 - core) * 16, 16)], kcr)
    loads[4].wait()
    for b in range(4):
        prod = jnp.dot(
            rk[8 * b : 8 * (b + 1)].reshape(128, KP), cx[...], preferred_element_type=F32
        )
        p[8 * b : 8 * (b + 1)] = (prod * apply_weight).astype(BF16).reshape(8, 16, NW)
    p_round(0)
    y_round(3)
    p_round(1)
    y_round(4)

    sp[...] = lax.dot_general(
        rn[slot_of(y, z)], rn[...].reshape(512, NW), NT, preferred_element_type=F32
    ).astype(BF16)
    send(sp, sq, scs, scr, col_dev(m * 2 + 1 - core))
    p_round(2)
    wait_for(sq, scr)
    sall[...] = (sp[...].astype(F32) + sq[...].astype(F32)).astype(BF16)
    for d in range(1, 8):
        send(sall, sr.at[d - 1], sms, smr, col_dev(((m + d) % 8) * 2 + core))

    rkt[...] = rk[...].reshape(512, KP).T
    factor = gram_weight / EXAMPLES
    for b in range(3):
        lines = pl.ds(pl.multiple_of(off + 192 * b, 64), 192)
        left = rkt[lines, :]
        for n in range(3):
            cols = slice(384 * n, 384 * (n + 1))
            gram = jnp.dot(left, rn[:, :, cols].reshape(512, 384), preferred_element_type=F32)
            new = cx[lines, cols].astype(F32) + gram * factor
            cn[192 * b : 192 * (b + 1), cols] = new.astype(BF16)
    out = pltpu.make_async_copy(cn, cn_hbm, out_sem)
    out.start()

    p_round(3)
    for j in range(NZ):
        for way in range(2):
            wait_for(rp.at[way, 3, j], rpr.at[way, 3, j])
        done = p[slot_of(y, j)].astype(F32)
        for way in range(2):
            done = done + rp[way, 3, j].astype(F32)
        zs[j] = done.astype(BF16)

        @pl.when(z != j)
        def _():
            send(zs.at[j], zr.at[(j - z + NZ) % NZ - 1], zrs, zrr, hid_dev(y, j))

    wait_for(sr, smr)
    s = sall[...].astype(F32)
    for d in range(7):
        s = s + sr[d].astype(F32)
    high = s.astype(BF16)
    low = (s - high.astype(F32)).astype(BF16)
    both = jnp.dot(
        jnp.concatenate([high, low], axis=0), rn[...].reshape(512, NW),
        preferred_element_type=F32,
    )
    final = (both[0:16] + both[16:32]) * (factor * apply_weight) + zs[z].astype(F32)
    wait_for(zr, zrr)
    for d in range(3):
        final = final + zr[d].astype(F32)
    app_ref[...] = final[0:OWN, :]

    wait_for(q1, q1s)
    wait_for(r1, a1s)
    wait_for(rn.at[pl.ds(0, 3)], zas)
    wait_for(rn.at[pl.ds(0, 28)], yas)
    wait_for(rk.at[pl.ds(0, 2)], khs)
    wait_for(rk.at[pl.ds(0, 12)], kxs)
    wait_for(rk.at[pl.ds(0, 16)], kcs)
    wait_for(rn.at[pl.ds(0, 28)], rps)
    wait_for(zr, zrs)
    wait_for(sp, scs)
    wait_for(sr, sms)

    @pl.when(is_root)
    def _():
        wait_for(rn.at[pl.ds(0, 15)], ns)
        wait_for(rk.at[pl.ds(0, 31)], ks)

    out.wait()


def per_device(inputs, out_grads, proj_in, proj_out, curvature):
    dma = pltpu.SemaphoreType.DMA
    vm = pltpu.VMEM
    hbm = pl.BlockSpec(memory_space=pl.ANY)
    return pl.pallas_call(
        kernel,
        out_shape=(
            jax.ShapeDtypeStruct((OWN, NW), F32),
            jax.ShapeDtypeStruct((KW, NW), BF16),
        ),
        in_specs=[hbm] * 5,
        out_specs=(pl.BlockSpec(memory_space=pltpu.VMEM), hbm),
        scratch_shapes=[
            vm(inputs.shape, BF16), vm(out_grads.shape, BF16), vm(proj_in.shape, BF16),
            vm(proj_out.shape, BF16), vm((KP, NW), BF16),
            vm((8, FEATS, 128), BF16), vm((3, 2, ZR, 128), BF16), vm((2, ZR, 128), BF16),
            vm((NY, 4, ZR, 128), BF16), vm((7, YR, 128), BF16), vm((YR, 128), BF16),
            vm((3, YR, 128), BF16), vm((YR, 128), BF16), vm((FEATS, 512), BF16),
            vm((PIN, 512), F32), vm((256, 512), BF16), vm((256, 512), BF16),
            vm((16, PIN * POUT), BF16),
            vm((32, 16, NW), BF16), vm((32, 16, KP), BF16), vm((KP, 512), BF16),
            vm((KW, NW), BF16), vm((32, 16, NW), BF16), vm((2, 4, 4, 16, NW), BF16),
            vm((4, 16, NW), BF16), vm((3, 16, NW), BF16),
            vm((16, 512), BF16), vm((16, 512), BF16), vm((7, 16, 512), BF16), vm((16, 512), BF16),
            dma((5,)), dma, dma, dma, dma, dma, dma, dma, dma, dma, dma, dma, dma, dma, dma,
            dma, dma((4,)), dma, dma((2, 4, 4)), dma, dma, dma, dma((3,)), dma, dma,
            dma, dma((2, 4, 4)), dma, dma, dma, dma, dma, dma, dma,
        ],
        compiler_params=pltpu.CompilerParams(
            collective_id=0, has_side_effects=True, vmem_limit_bytes=60 * 2**20
        ),
    )(inputs, out_grads, proj_in, proj_out, curvature)


def solution(mesh):
    in_specs = (P("col", "hid"), P("col", "hid"), P(None, "hid"), P(None, "hid"), P("hid", "col"))
    out_specs = (P("hid", "col"), P("hid", "col"))
    return jax.shard_map(
        per_device, mesh=mesh, in_specs=in_specs, out_specs=out_specs, check_vma=False
    )
```

```python
import jax
import jax.numpy as jnp
from jax import lax
from jax.experimental import pallas as pl
from jax.experimental.pallas import tpu as pltpu
from jax.sharding import PartitionSpec as P

MESH = pl.DeviceIdType.MESH
F32 = jnp.float32
BF16 = jnp.bfloat16

PIN = 96
POUT = 192
FEATS = PIN + POUT
ZR = 96
YR = FEATS - ZR
SEQ = 32
EXAMPLES = 480
NY, NZ = 8, 4
N_HID, N_COL = 32, 16
OWN = 15
TOK = OWN * SEQ
NW = 1152
KW = 576
KP = 640
gram_weight = 1.0 / 64.0
apply_weight = 1.0 / 16.0
NT = (((1,), (1,)), ((), ()))


def slot_of(y, z):
    return (z // 2) * 16 + y * 2 + z % 2


def root_group(y, z):
    return (y + 16 - 4 * (z % 2) - 2 * (z // 2)) % NY


def block_slot(y, z):
    return slot_of(root_group(y, z), z)


def kernel(
    x_hbm, g_hbm, wi_hbm, wo_hbm, c_hbm,
    app_ref, cn_out,
    xv, gv, wiv, wov, cx,
    part, q1, qs, q2, r1, s1, r2, s2, r3, featv, ge, go, rows,
    rn, rk, rkt, p, rp, zs, zr, sp, sq, sr, sall,
    in_sem, q1s, q1r, q2s, q2r, a1s, a1r, a2s, a2r, a3s, a3r, ns, nr, ks, kr,
    zas, zar, yas, yar, khs, khr, kxs, kxr, kcs, kcr,
    rps, rpr, zrs, zrr, scs, scr, sms, smr,
):
    h = lax.axis_index("hid")
    c = lax.axis_index("col")
    y, z = h // NZ, h % NZ
    core = c % 2
    m = c // 2
    x, zh = m // 2, m % 2
    first_y = (m + 2 * core + NY - 1) % NY

    def chunk_of(yy):
        return (yy + NY - first_y) % NY

    z_target = 2 * core + chunk_of(y) // 4
    y_root = (m + 4 * (z % 2) + 2 * (z // 2)) % NY
    is_target = z == z_target
    is_root = jnp.logical_and(y == y_root, core == z // 2)
    own_slot = block_slot(y, z)

    def hid_dev(yy, zz):
        return (yy * NZ + zz, c)

    def col_dev(cc):
        return (h, cc)

    def send(src, dst, ssem, rsem, dev):
        copy = pltpu.make_async_remote_copy(
            src_ref=src, dst_ref=dst, send_sem=ssem, recv_sem=rsem,
            device_id=dev, device_id_type=MESH,
        )
        copy.start()

    def wait_for(ref, sem):
        pltpu.make_async_copy(ref, ref, sem).wait()

    off = pl.multiple_of(64 * (h % 2), 64)
    loads = []
    for i, (src, dst) in enumerate(
        (
            (x_hbm, xv), (wi_hbm, wiv), (g_hbm, gv), (wo_hbm, wov),
            (c_hbm, cx.at[pl.ds(off, KW)]),
        )
    ):
        load = pltpu.make_async_copy(src, dst, in_sem.at[i])
        load.start()
        loads.append(load)

    barrier = pltpu.get_barrier_semaphore()

    def greet(dev):
        pl.semaphore_signal(barrier, inc=1, device_id=dev, device_id_type=MESH)

    for d in range(1, NY):
        greet(hid_dev((y + d) % NY, z))
    for d in range(1, NZ):
        greet(hid_dev(y, (z + d) % NZ))
    zh_c = (x * 2 + (1 - zh)) * 2 + core
    greet(col_dev(zh_c))
    for d in range(1, 4):
        greet(col_dev((((x + d) % 4) * 2 + zh) * 2 + core))
    greet(col_dev(m * 2 + 1 - core))

    @pl.when(jnp.logical_not(is_root))
    def _():
        greet(col_dev(root_group(y, z) * 2 + z // 2))

    zero_tail = jnp.zeros((FEATS, 128), BF16)
    for hf in range(2):
        part[4 * hf + 3] = zero_tail
    loads[2].wait()
    loads[3].wait()

    def project(w, v, first):
        for hf in range(2):
            t = lax.dot_general(
                w[...], v[TOK * hf : TOK * (hf + 1), :], NT, preferred_element_type=F32
            ).astype(BF16)
            n = t.shape[0]
            for q in range(3):
                part[4 * hf + q, first : first + n, :] = t[:, 128 * q : 128 * (q + 1)]
            part[4 * hf + 3, first : first + n, 0:96] = t[:, 384:480]

    project(wov, gv, 0)
    loads[0].wait()
    loads[1].wait()
    project(wiv, xv, POUT)

    pl.semaphore_wait(barrier, jnp.where(is_root, 30, 15))

    z_first = pl.ds(0, ZR)
    y_first = pl.ds(ZR, YR)
    for d in (2, 1, 3):
        zz = (z + d) % NZ
        send(part.at[pl.ds(2 * zz, 2), z_first], q1.at[d - 1], q1s, q1r, hid_dev(y, zz))
    for d in (4, 3, 5, 2, 6, 1, 7):
        yy = (y + d) % NY
        send(part.at[chunk_of(yy), y_first], r1.at[d - 1], a1s, a1r, hid_dev(yy, z))
    cx[pl.ds(pl.multiple_of(KW * (1 - h % 2), 64), 64), :] = jnp.zeros((64, NW), BF16)

    wait_for(q1, q1r)
    both = part[pl.ds(2 * z, 2), 0:ZR].astype(F32)
    for d in range(3):
        both = both + q1[d].astype(F32)
    qs[...] = both.astype(BF16)
    q_z = 2 * core + z // 2
    q_y = (m + 4 * (z // 2) + 2 * core) % NY
    q_place = q2.at[y, pl.ds(2 * (z % 2), 2)]
    q_here = jnp.logical_and(q_y == y, q_z == z)

    @pl.when(q_here)
    def _():
        pltpu.make_async_copy(qs, q_place, q2r).start()

    @pl.when(jnp.logical_not(q_here))
    def _():
        send(qs, q_place, q2s, q2r, hid_dev(q_y, q_z))

    wait_for(r1, a1r)
    total = part[chunk_of(y), ZR:FEATS].astype(F32)
    for d in range(7):
        total = total + r1[d].astype(F32)
    s1[...] = total.astype(BF16)

    @pl.when(jnp.logical_not(is_target))
    def _():
        send(s1, r2.at[(z - z_target + NZ) % NZ - 1], a2s, a2r, hid_dev(y, z_target))
        wait_for(s1, a2s)

    @pl.when(is_target)
    def _():
        wait_for(r2, a2r)
        whole = s1[...].astype(F32)
        for d in range(3):
            whole = whole + r2[d].astype(F32)
        s2[...] = whole.astype(BF16)
        place = r3.at[y_first, pl.ds(pl.multiple_of(128 * (chunk_of(y) % 4), 128), 128)]

        @pl.when(y != y_root)
        def _():
            send(s2, place, a3s, a3r, hid_dev(y_root, z))
            wait_for(s2, a3s)

        @pl.when(y == y_root)
        def _():
            pltpu.make_async_copy(s2, place, a3r).start()

    @pl.when(jnp.logical_not(q_here))
    def _():
        wait_for(qs, q2s)

    k_base = core * 16 + m * 2

    @pl.when(is_root)
    def _():
        wait_for(q2, q2r)
        for t in range(4):
            summed = q2[0, t].astype(F32)
            for d in range(1, NY):
                summed = summed + q2[d, t].astype(F32)
            r3[0:ZR, 128 * t : 128 * (t + 1)] = summed.astype(BF16)
        wait_for(r3.at[y_first], a3r)
        ge[0:POUT, :] = r3[0:POUT, :]
        ge[POUT:256, :] = jnp.zeros((64, 512), BF16)
        go[0:64, :] = jnp.zeros((64, 512), BF16)
        go[64:256, :] = r3[0:POUT, :]
        featv[...] = r3[POUT:FEATS, :].astype(F32)
        mine = (
            lax.broadcasted_iota(jnp.int32, (16, 512), 1) // SEQ
            == lax.broadcasted_iota(jnp.int32, (16, 512), 0)
        )

        def form(i, carry):
            def spread(odd):
                return jnp.concatenate(
                    [
                        jnp.where(
                            mine,
                            jnp.broadcast_to(featv[pl.ds(i * 24 + 2 * q + odd, 1), :], (16, 512)),
                            0.0,
                        ).astype(BF16)
                        for q in range(12)
                    ],
                    axis=0,
                )

            even = lax.dot_general(spread(0), ge[...], NT, preferred_element_type=F32)
            odd = lax.dot_general(spread(1), go[...], NT, preferred_element_type=F32)
            for q in range(12):
                e = even[16 * q : 16 * (q + 1)]
                o = odd[16 * q : 16 * (q + 1)]
                three = jnp.concatenate(
                    [e[:, 0:128], e[:, 128:256] + o[:, 0:128], o[:, 128:256]], axis=1
                )
                at = pl.multiple_of(i * 4608 + 384 * q, 128)
                rows[:, pl.ds(at, 384)] = three.astype(BF16)
            return carry

        lax.fori_loop(0, 4, form, 0)

        def n_slice(cc):
            return rows.at[:, pl.ds(pl.multiple_of(cc * NW, 128), NW)]

        def k_slice(kk):
            return rows.at[:, pl.ds(pl.multiple_of((kk // 2) * NW + (kk % 2) * 512, 128), KP)]

        pltpu.make_async_copy(n_slice(c), rn.at[own_slot], nr).start()
        pltpu.make_async_copy(k_slice(h), rk.at[own_slot], kr).start()

        def to_col(dx, dz, dc):
            cc = (((x + dx) % 4) * 2 + (zh + dz) % 2) * 2 + (core + dc) % 2
            send(n_slice(cc), rn.at[own_slot], ns, nr, col_dev(cc))

        def to_hid(dy, dz):
            kk = ((y + dy) % NY) * NZ + (z + dz) % NZ
            send(k_slice(kk), rk.at[own_slot], ks, kr, (kk, c))

        for dx in (2, 1, 3, 0):
            for dc in range(2):
                to_col(dx, 1, dc)
        for dy in (4, 3, 5, 2, 6, 1, 7, 0):
            for dz in range(NZ):
                if dy + dz > 0:
                    to_hid(dy, dz)
        for dx in (2, 1, 3, 0):
            for dc in range(2):
                if dx + dc > 0:
                    to_col(dx, 0, dc)

    up, down = (y + 1) % NY, (y + NY - 1) % NY

    def y_block(hop, way, j):
        yy = (y - hop + NY) % NY if way == 0 else (y + hop) % NY
        return rn.at[block_slot(yy, (z + j) % NZ)]

    def y_hops(way, j):
        return 4 if (j < 2) == (way == 0) else 3

    def y_send(hop, way, j):
        block = y_block(hop, way, j)
        send(block, block, yas, yar.at[way, hop, j], hid_dev(up if way == 0 else down, z))

    wait_for(rn.at[own_slot], nr)
    for way in range(2):
        y_send(0, way, 0)
    for d in range(1, NZ):
        send(rn.at[own_slot], rn.at[own_slot], zas, zar.at[NZ - d], hid_dev(y, (z + d) % NZ))
    wait_for(rk.at[pl.ds(k_base, 2)], kr)
    k_two = rk.at[pl.ds(k_base, 2)]
    send(k_two, k_two, khs, khr, col_dev(zh_c))
    for j in range(1, NZ):
        wait_for(rn.at[block_slot(y, (z + j) % NZ)], zar.at[j])
        for way in range(2):
            y_send(0, way, j)

    def y_round(hop):
        for j in range(NZ):
            for way in range(2):
                if hop <= y_hops(way, j):
                    wait_for(y_block(hop, way, j), yar.at[way, hop - 1, j])
                    if hop < y_hops(way, j):
                        y_send(hop, way, j)

    def p_slot(left_hops, way, j):
        yy = (y + left_hops) % NY if way == 0 else (y - left_hops + NY) % NY
        return slot_of(yy, (2 * core + j) % NZ)

    def p_round(step, which=range(NZ)):
        for j in which:
            for way in range(2):
                hops = y_hops(way, j)
                left = 4 - step
                if left > hops:
                    continue
                at = p_slot(left, way, j)
                if left == hops:
                    src = p.at[at]
                else:
                    src = rp.at[way, step - 1, j]
                    wait_for(src, rpr.at[way, step - 1, j])
                    src[...] = (src[...].astype(F32) + p[at].astype(F32)).astype(BF16)
                send(src, rp.at[way, step, j], rps, rpr.at[way, step, j],
                     hid_dev(up if way == 0 else down, z))

    wait_for(rk.at[pl.ds(core * 16 + x * 4 + (1 - zh) * 2, 2)], khr)
    k_four = rk.at[pl.ds(core * 16 + x * 4, 4)]
    for d in range(1, 4):
        xx = (x + d) % 4
        send(k_four, k_four, kxs, kxr.at[d - 1], col_dev((xx * 2 + zh) * 2 + core))
    y_round(1)
    for d in range(1, 4):
        wait_for(rk.at[pl.ds(core * 16 + ((x + 4 - d) % 4) * 4, 4)], kxr.at[d - 1])
    k_all = rk.at[pl.ds(core * 16, 16)]
    send(k_all, k_all, kcs, kcr, col_dev(m * 2 + 1 - core))
    y_round(2)
    loads[4].wait()

    def product(half):
        for b in range(2):
            at = pl.ds(half * 16 + 8 * b, 8)
            prod = jnp.dot(
                rk[at].reshape(128, KP), cx[...], preferred_element_type=F32
            )
            p[at] = (prod * apply_weight).astype(BF16).reshape(8, 16, NW)

    product(core)
    p_round(0, (0, 1))
    wait_for(rk.at[pl.ds((1 - core) * 16, 16)], kcr)
    product(1 - core)
    p_round(0, (2, 3))
    y_round(3)
    p_round(1)
    y_round(4)

    sp[...] = lax.dot_general(
        rn[slot_of(y, z)], rn[...].reshape(512, NW), NT, preferred_element_type=F32
    ).astype(BF16)
    send(sp, sq, scs, scr, col_dev(m * 2 + 1 - core))
    p_round(2)
    wait_for(sq, scr)
    sall[...] = (sp[...].astype(F32) + sq[...].astype(F32)).astype(BF16)
    for d in range(1, 8):
        send(sall, sr.at[d - 1], sms, smr, col_dev(((m + d) % 8) * 2 + core))

    p_round(3)

    rkt[...] = rk[...].reshape(512, KP).T
    factor = gram_weight / EXAMPLES
    for b in range(3):
        lines = pl.ds(pl.multiple_of(off + 192 * b, 64), 192)
        left = rkt[lines, :]
        for n in range(3):
            cols = slice(384 * n, 384 * (n + 1))
            gram = jnp.dot(left, rn[:, :, cols].reshape(512, 384), preferred_element_type=F32)
            new = cx[lines, cols].astype(F32) + gram * factor
            cn_out[192 * b : 192 * (b + 1), cols] = new.astype(BF16)

    for j in range(NZ):
        zz = (2 * core + j) % NZ
        for way in range(2):
            wait_for(rp.at[way, 3, j], rpr.at[way, 3, j])
        done = p[slot_of(y, zz)].astype(F32)
        for way in range(2):
            done = done + rp[way, 3, j].astype(F32)
        zs[j] = done.astype(BF16)

        @pl.when(z != zz)
        def _():
            send(zs.at[j], zr.at[(zz - z + NZ) % NZ - 1], zrs, zrr, hid_dev(y, zz))

    wait_for(sr, smr)
    s = sall[...].astype(F32)
    for d in range(7):
        s = s + sr[d].astype(F32)
    high = s.astype(BF16)
    low = (s - high.astype(F32)).astype(BF16)
    both = jnp.dot(
        jnp.concatenate([high, low], axis=0), rn[...].reshape(512, NW),
        preferred_element_type=F32,
    )
    final = (both[0:16] + both[16:32]) * (factor * apply_weight) + zs[(z + NZ - 2 * core) % NZ].astype(F32)
    wait_for(zr, zrr)
    for d in range(3):
        final = final + zr[d].astype(F32)
    app_ref[...] = final[0:OWN, :]

    wait_for(q1, q1s)
    wait_for(r1, a1s)
    wait_for(rn.at[pl.ds(0, 3)], zas)
    wait_for(rn.at[pl.ds(0, 28)], yas)
    wait_for(rk.at[pl.ds(0, 2)], khs)
    wait_for(rk.at[pl.ds(0, 12)], kxs)
    wait_for(rk.at[pl.ds(0, 16)], kcs)
    wait_for(rn.at[pl.ds(0, 28)], rps)
    wait_for(zr, zrs)
    wait_for(sp, scs)
    wait_for(sr, sms)

    @pl.when(is_root)
    def _():
        wait_for(rn.at[pl.ds(0, 15)], ns)
        wait_for(rk.at[pl.ds(0, 31)], ks)


def hand_over(app_in, cn_in, app_out, cn_out, sem):
    copies = [pltpu.make_async_copy(app_in, app_out, sem.at[4])]
    for i in range(4):
        lines = pl.ds(144 * i, 144)
        copies.append(pltpu.make_async_copy(cn_in.at[lines], cn_out.at[lines], sem.at[i]))
    for copy in copies:
        copy.start()
    for copy in copies:
        copy.wait()


def per_device(inputs, out_grads, proj_in, proj_out, curvature):
    dma = pltpu.SemaphoreType.DMA
    vm = pltpu.VMEM
    hbm = pl.BlockSpec(memory_space=pl.ANY)
    applied, curvature_new = pl.pallas_call(
        kernel,
        out_shape=(
            pltpu.VMEM((OWN, NW), F32),
            pltpu.VMEM((KW, NW), BF16),
        ),
        in_specs=[hbm] * 5,
        out_specs=(pl.BlockSpec(memory_space=pltpu.VMEM),) * 2,
        scratch_shapes=[
            vm(inputs.shape, BF16), vm(out_grads.shape, BF16), vm(proj_in.shape, BF16),
            vm(proj_out.shape, BF16), vm((KP, NW), BF16),
            vm((8, FEATS, 128), BF16), vm((3, 2, ZR, 128), BF16), vm((2, ZR, 128), BF16),
            vm((NY, 4, ZR, 128), BF16), vm((7, YR, 128), BF16), vm((YR, 128), BF16),
            vm((3, YR, 128), BF16), vm((YR, 128), BF16), vm((FEATS, 512), BF16),
            vm((PIN, 512), F32), vm((256, 512), BF16), vm((256, 512), BF16),
            vm((16, PIN * POUT), BF16),
            vm((32, 16, NW), BF16), vm((32, 16, KP), BF16), vm((KP, 512), BF16),
            vm((32, 16, NW), BF16), vm((2, 4, 4, 16, NW), BF16),
            vm((4, 16, NW), BF16), vm((3, 16, NW), BF16),
            vm((16, 512), BF16), vm((16, 512), BF16), vm((7, 16, 512), BF16), vm((16, 512), BF16),
            dma((5,)), dma, dma, dma, dma, dma, dma, dma, dma, dma, dma, dma, dma, dma, dma,
            dma, dma((4,)), dma, dma((2, 4, 4)), dma, dma, dma, dma((3,)), dma, dma,
            dma, dma((2, 4, 4)), dma, dma, dma, dma, dma, dma,
        ],
        compiler_params=pltpu.CompilerParams(
            collective_id=0, has_side_effects=True, vmem_limit_bytes=48 * 2**20
        ),
    )(*(
        pltpu.with_memory_space_constraint(a, pltpu.HBM)
        for a in (inputs, out_grads, proj_in, proj_out, curvature)
    ))
    return pl.pallas_call(
        hand_over,
        out_shape=(
            jax.ShapeDtypeStruct((OWN, NW), F32),
            jax.ShapeDtypeStruct((KW, NW), BF16),
        ),
        in_specs=[hbm] * 2,
        out_specs=(hbm, hbm),
        scratch_shapes=[dma((5,))],
        compiler_params=pltpu.CompilerParams(vmem_limit_bytes=2 * 2**20),
    )(applied, curvature_new)


def solution(mesh):
    in_specs = (P("col", "hid"), P("col", "hid"), P(None, "hid"), P(None, "hid"), P("hid", "col"))
    out_specs = (P("hid", "col"), P("hid", "col"))
    return jax.shard_map(
        per_device, mesh=mesh, in_specs=in_specs, out_specs=out_specs, check_vma=False
    )
```

```python
import jax
import jax.numpy as jnp
from jax import lax
from jax.experimental import pallas as pl
from jax.experimental.pallas import tpu as pltpu
from jax.sharding import PartitionSpec as P

MESH = pl.DeviceIdType.MESH
F32 = jnp.float32
BF16 = jnp.bfloat16

PIN = 96
POUT = 192
FEATS = PIN + POUT
ZR = 112
YR = FEATS - ZR
SEQ = 32
EXAMPLES = 480
NY, NZ = 8, 4
N_HID, N_COL = 32, 16
OWN = 15
TOK = OWN * SEQ
NW = 1152
KW = 576
KP = 640
gram_weight = 1.0 / 64.0
apply_weight = 1.0 / 16.0
NT = (((1,), (1,)), ((), ()))


def slot_of(y, z):
    return (z // 2) * 16 + y * 2 + z % 2


def root_group(y, z):
    return (y + 16 - 4 * (z % 2) - 2 * (z // 2)) % NY


def block_slot(y, z):
    return slot_of(root_group(y, z), z)


def kernel(
    x_hbm, g_hbm, wi_hbm, wo_hbm, c_hbm,
    app_ref, cn_out,
    xv, gv, wiv, wov, cx,
    part, q1, qs, q2, r1, s1, r2, s2, r3, featv, ge, go, rows,
    rn, rk, rkt, p, rp, zs, zr, sp, sq, sr, sall,
    in_sem, q1s, q1r, q2s, q2r, a1s, a1r, a2s, a2r, a3s, a3r, ns, nr, ks, kr,
    zas, zar, yas, yar, khs, khr, kxs, kxr, kcs, kcr,
    rps, rpr, zrs, zrr, scs, scr, sms, smr,
):
    h = lax.axis_index("hid")
    c = lax.axis_index("col")
    y, z = h // NZ, h % NZ
    core = c % 2
    m = c // 2
    x, zh = m // 2, m % 2
    first_y = (m + 2 * core + NY - 1) % NY

    def chunk_of(yy):
        return (yy + NY - first_y) % NY

    z_target = 2 * core + chunk_of(y) // 4
    y_root = (m + 4 * (z % 2) + 2 * (z // 2)) % NY
    is_target = z == z_target
    is_root = jnp.logical_and(y == y_root, core == z // 2)
    own_slot = block_slot(y, z)

    def hid_dev(yy, zz):
        return (yy * NZ + zz, c)

    def col_dev(cc):
        return (h, cc)

    def send(src, dst, ssem, rsem, dev):
        copy = pltpu.make_async_remote_copy(
            src_ref=src, dst_ref=dst, send_sem=ssem, recv_sem=rsem,
            device_id=dev, device_id_type=MESH,
        )
        copy.start()

    def wait_for(ref, sem):
        pltpu.make_async_copy(ref, ref, sem).wait()

    off = pl.multiple_of(64 * (h % 2), 64)
    loads = []
    for i, (src, dst) in enumerate(
        (
            (x_hbm, xv), (wi_hbm, wiv), (g_hbm, gv), (wo_hbm, wov),
            (c_hbm, cx.at[pl.ds(off, KW)]),
        )
    ):
        load = pltpu.make_async_copy(src, dst, in_sem.at[i])
        load.start()
        loads.append(load)

    barrier = pltpu.get_barrier_semaphore()

    def greet(dev):
        pl.semaphore_signal(barrier, inc=1, device_id=dev, device_id_type=MESH)

    for d in range(1, NY):
        greet(hid_dev((y + d) % NY, z))
    for d in range(1, NZ):
        greet(hid_dev(y, (z + d) % NZ))
    zh_c = (x * 2 + (1 - zh)) * 2 + core
    greet(col_dev(zh_c))
    for d in range(1, 4):
        greet(col_dev((((x + d) % 4) * 2 + zh) * 2 + core))
    greet(col_dev(m * 2 + 1 - core))

    @pl.when(jnp.logical_not(is_root))
    def _():
        greet(col_dev(root_group(y, z) * 2 + z // 2))

    zero_tail = jnp.zeros((FEATS, 128), BF16)
    for hf in range(2):
        part[4 * hf + 3] = zero_tail
    loads[2].wait()
    loads[3].wait()

    def project(w, v, first):
        for hf in range(2):
            t = lax.dot_general(
                w[...], v[TOK * hf : TOK * (hf + 1), :], NT, preferred_element_type=F32
            ).astype(BF16)
            n = t.shape[0]
            for q in range(3):
                part[4 * hf + q, first : first + n, :] = t[:, 128 * q : 128 * (q + 1)]
            part[4 * hf + 3, first : first + n, 0:96] = t[:, 384:480]

    project(wov, gv, 0)
    loads[0].wait()
    loads[1].wait()
    project(wiv, xv, POUT)

    pl.semaphore_wait(barrier, jnp.where(is_root, 30, 15))

    z_first = pl.ds(0, ZR)
    y_first = pl.ds(ZR, YR)
    for d in (2, 1, 3):
        zz = (z + d) % NZ
        send(part.at[pl.ds(2 * zz, 2), z_first], q1.at[d - 1], q1s, q1r, hid_dev(y, zz))
    for d in (4, 3, 5, 2, 6, 1, 7):
        yy = (y + d) % NY
        send(part.at[chunk_of(yy), y_first], r1.at[d - 1], a1s, a1r, hid_dev(yy, z))
    cx[pl.ds(pl.multiple_of(KW * (1 - h % 2), 64), 64), :] = jnp.zeros((64, NW), BF16)

    wait_for(q1, q1r)
    both = part[pl.ds(2 * z, 2), 0:ZR].astype(F32)
    for d in range(3):
        both = both + q1[d].astype(F32)
    qs[...] = both.astype(BF16)
    q_z = 2 * core + z // 2
    q_y = (m + 4 * (z // 2) + 2 * core) % NY
    q_place = q2.at[y, pl.ds(2 * (z % 2), 2)]
    q_here = jnp.logical_and(q_y == y, q_z == z)

    @pl.when(q_here)
    def _():
        pltpu.make_async_copy(qs, q_place, q2r).start()

    @pl.when(jnp.logical_not(q_here))
    def _():
        send(qs, q_place, q2s, q2r, hid_dev(q_y, q_z))

    wait_for(r1, a1r)
    total = part[chunk_of(y), ZR:FEATS].astype(F32)
    for d in range(7):
        total = total + r1[d].astype(F32)
    s1[...] = total.astype(BF16)

    @pl.when(jnp.logical_not(is_target))
    def _():
        send(s1, r2.at[(z - z_target + NZ) % NZ - 1], a2s, a2r, hid_dev(y, z_target))
        wait_for(s1, a2s)

    @pl.when(is_target)
    def _():
        wait_for(r2, a2r)
        whole = s1[...].astype(F32)
        for d in range(3):
            whole = whole + r2[d].astype(F32)
        s2[...] = whole.astype(BF16)
        place = r3.at[y_first, pl.ds(pl.multiple_of(128 * (chunk_of(y) % 4), 128), 128)]

        @pl.when(y != y_root)
        def _():
            send(s2, place, a3s, a3r, hid_dev(y_root, z))
            wait_for(s2, a3s)

        @pl.when(y == y_root)
        def _():
            pltpu.make_async_copy(s2, place, a3r).start()

    @pl.when(jnp.logical_not(q_here))
    def _():
        wait_for(qs, q2s)

    k_base = core * 16 + m * 2

    @pl.when(is_root)
    def _():
        wait_for(q2, q2r)
        for t in range(4):
            summed = q2[0, t].astype(F32)
            for d in range(1, NY):
                summed = summed + q2[d, t].astype(F32)
            r3[0:ZR, 128 * t : 128 * (t + 1)] = summed.astype(BF16)
        wait_for(r3.at[y_first], a3r)
        ge[0:POUT, :] = r3[0:POUT, :]
        ge[POUT:256, :] = jnp.zeros((64, 512), BF16)
        go[0:64, :] = jnp.zeros((64, 512), BF16)
        go[64:256, :] = r3[0:POUT, :]
        featv[...] = r3[POUT:FEATS, :].astype(F32)
        mine = (
            lax.broadcasted_iota(jnp.int32, (16, 512), 1) // SEQ
            == lax.broadcasted_iota(jnp.int32, (16, 512), 0)
        )

        def n_slice(cc):
            return rows.at[:, pl.ds(pl.multiple_of(cc * NW, 128), NW)]

        def k_slice(kk):
            return rows.at[:, pl.ds(pl.multiple_of((kk // 2) * NW + (kk % 2) * 512, 128), KP)]

        def to_col(cc):
            @pl.when(cc != c)
            def _():
                send(n_slice(cc), rn.at[own_slot], ns, nr, col_dev(cc))

            @pl.when(cc == c)
            def _():
                pltpu.make_async_copy(n_slice(cc), rn.at[own_slot], nr).start()

        def to_hid(kk):
            @pl.when(kk != h)
            def _():
                send(k_slice(kk), rk.at[own_slot], ks, kr, (kk, c))

            @pl.when(kk == h)
            def _():
                pltpu.make_async_copy(k_slice(kk), rk.at[own_slot], kr).start()

        def form(step, carry):
            i = (x + 3 - step) % 4
            def spread(odd):
                return jnp.concatenate(
                    [
                        jnp.where(
                            mine,
                            jnp.broadcast_to(featv[pl.ds(i * 24 + 2 * q + odd, 1), :], (16, 512)),
                            0.0,
                        ).astype(BF16)
                        for q in range(12)
                    ],
                    axis=0,
                )

            even = lax.dot_general(spread(0), ge[...], NT, preferred_element_type=F32)
            odd = lax.dot_general(spread(1), go[...], NT, preferred_element_type=F32)
            for q in range(12):
                e = even[16 * q : 16 * (q + 1)]
                o = odd[16 * q : 16 * (q + 1)]
                three = jnp.concatenate(
                    [e[:, 0:128], e[:, 128:256] + o[:, 0:128], o[:, 128:256]], axis=1
                )
                at = pl.multiple_of(i * 4608 + 384 * q, 128)
                rows[:, pl.ds(at, 384)] = three.astype(BF16)
            for dc in range(2):
                to_col(4 * i + 2 * (1 - zh) + dc)
            for dk in range(8):
                to_hid(8 * i + dk)
            for dc in range(2):
                to_col(4 * i + 2 * zh + dc)
            return carry

        lax.fori_loop(0, 4, form, 0)

    up, down = (y + 1) % NY, (y + NY - 1) % NY

    def y_block(hop, way, j):
        yy = (y - hop + NY) % NY if way == 0 else (y + hop) % NY
        return rn.at[block_slot(yy, (z + j) % NZ)]

    def y_hops(way, j):
        return 4 if (j < 2) == (way == 0) else 3

    def y_send(hop, way, j):
        block = y_block(hop, way, j)
        send(block, block, yas, yar.at[way, hop, j], hid_dev(up if way == 0 else down, z))

    wait_for(rn.at[own_slot], nr)
    for way in range(2):
        y_send(0, way, 0)
    for d in range(1, NZ):
        send(rn.at[own_slot], rn.at[own_slot], zas, zar.at[NZ - d], hid_dev(y, (z + d) % NZ))
    wait_for(rk.at[pl.ds(k_base, 2)], kr)
    k_two = rk.at[pl.ds(k_base, 2)]
    send(k_two, k_two, khs, khr, col_dev(zh_c))
    for j in range(1, NZ):
        wait_for(rn.at[block_slot(y, (z + j) % NZ)], zar.at[j])
        for way in range(2):
            y_send(0, way, j)

    def y_round(hop):
        for j in range(NZ):
            for way in range(2):
                if hop <= y_hops(way, j):
                    wait_for(y_block(hop, way, j), yar.at[way, hop - 1, j])
                    if hop < y_hops(way, j):
                        y_send(hop, way, j)

    def p_slot(left_hops, way, j):
        yy = (y + left_hops) % NY if way == 0 else (y - left_hops + NY) % NY
        return slot_of(yy, (2 * core + j) % NZ)

    def p_round(step, which=range(NZ)):
        for j in which:
            for way in range(2):
                hops = y_hops(way, j)
                left = 4 - step
                if left > hops:
                    continue
                at = p_slot(left, way, j)
                if left == hops:
                    src = p.at[at]
                else:
                    src = rp.at[way, step - 1, j]
                    wait_for(src, rpr.at[way, step - 1, j])
                    src[...] = (src[...].astype(F32) + p[at].astype(F32)).astype(BF16)
                send(src, rp.at[way, step, j], rps, rpr.at[way, step, j],
                     hid_dev(up if way == 0 else down, z))

    wait_for(rk.at[pl.ds(core * 16 + x * 4 + (1 - zh) * 2, 2)], khr)
    k_four = rk.at[pl.ds(core * 16 + x * 4, 4)]
    for d in range(1, 4):
        xx = (x + d) % 4
        send(k_four, k_four, kxs, kxr.at[d - 1], col_dev((xx * 2 + zh) * 2 + core))
    y_round(1)
    for d in range(1, 4):
        wait_for(rk.at[pl.ds(core * 16 + ((x + 4 - d) % 4) * 4, 4)], kxr.at[d - 1])
    k_all = rk.at[pl.ds(core * 16, 16)]
    send(k_all, k_all, kcs, kcr, col_dev(m * 2 + 1 - core))
    y_round(2)
    loads[4].wait()

    def product(half):
        for b in range(2):
            at = pl.ds(half * 16 + 8 * b, 8)
            prod = jnp.dot(
                rk[at].reshape(128, KP), cx[...], preferred_element_type=F32
            )
            p[at] = (prod * apply_weight).astype(BF16).reshape(8, 16, NW)

    product(core)
    p_round(0, (0, 1))
    wait_for(rk.at[pl.ds((1 - core) * 16, 16)], kcr)
    product(1 - core)
    p_round(0, (2, 3))
    y_round(3)
    p_round(1)
    y_round(4)

    sp[...] = lax.dot_general(
        rn[slot_of(y, z)], rn[...].reshape(512, NW), NT, preferred_element_type=F32
    ).astype(BF16)
    send(sp, sq, scs, scr, col_dev(m * 2 + 1 - core))
    p_round(2)
    wait_for(sq, scr)
    sall[...] = (sp[...].astype(F32) + sq[...].astype(F32)).astype(BF16)
    for d in range(1, 8):
        send(sall, sr.at[d - 1], sms, smr, col_dev(((m + d) % 8) * 2 + core))

    p_round(3)

    rkt[...] = rk[...].reshape(512, KP).T
    factor = gram_weight / EXAMPLES
    for b in range(3):
        lines = pl.ds(pl.multiple_of(off + 192 * b, 64), 192)
        left = rkt[lines, :]
        for n in range(3):
            cols = slice(384 * n, 384 * (n + 1))
            gram = jnp.dot(left, rn[:, :, cols].reshape(512, 384), preferred_element_type=F32)
            new = cx[lines, cols].astype(F32) + gram * factor
            cn_out[192 * b : 192 * (b + 1), cols] = new.astype(BF16)

    for j in range(NZ):
        zz = (2 * core + j) % NZ
        for way in range(2):
            wait_for(rp.at[way, 3, j], rpr.at[way, 3, j])
        done = p[slot_of(y, zz)].astype(F32)
        for way in range(2):
            done = done + rp[way, 3, j].astype(F32)
        zs[j] = done.astype(BF16)

        @pl.when(z != zz)
        def _():
            send(zs.at[j], zr.at[(zz - z + NZ) % NZ - 1], zrs, zrr, hid_dev(y, zz))

    wait_for(sr, smr)
    s = sall[...].astype(F32)
    for d in range(7):
        s = s + sr[d].astype(F32)
    high = s.astype(BF16)
    low = (s - high.astype(F32)).astype(BF16)
    both = jnp.dot(
        jnp.concatenate([high, low], axis=0), rn[...].reshape(512, NW),
        preferred_element_type=F32,
    )
    final = (both[0:16] + both[16:32]) * (factor * apply_weight) + zs[(z + NZ - 2 * core) % NZ].astype(F32)
    wait_for(zr, zrr)
    for d in range(3):
        final = final + zr[d].astype(F32)
    app_ref[...] = final[0:OWN, :]

    wait_for(q1, q1s)
    wait_for(r1, a1s)
    wait_for(rn.at[pl.ds(0, 3)], zas)
    wait_for(rn.at[pl.ds(0, 28)], yas)
    wait_for(rk.at[pl.ds(0, 2)], khs)
    wait_for(rk.at[pl.ds(0, 12)], kxs)
    wait_for(rk.at[pl.ds(0, 16)], kcs)
    wait_for(rn.at[pl.ds(0, 28)], rps)
    wait_for(zr, zrs)
    wait_for(sp, scs)
    wait_for(sr, sms)

    @pl.when(is_root)
    def _():
        wait_for(rn.at[pl.ds(0, 15)], ns)
        wait_for(rk.at[pl.ds(0, 31)], ks)


def hand_over(app_in, cn_in, app_out, cn_out, sem):
    copies = [pltpu.make_async_copy(app_in, app_out, sem.at[4])]
    for i in range(4):
        lines = pl.ds(144 * i, 144)
        copies.append(pltpu.make_async_copy(cn_in.at[lines], cn_out.at[lines], sem.at[i]))
    for copy in copies:
        copy.start()
    for copy in copies:
        copy.wait()


def per_device(inputs, out_grads, proj_in, proj_out, curvature):
    dma = pltpu.SemaphoreType.DMA
    vm = pltpu.VMEM
    hbm = pl.BlockSpec(memory_space=pl.ANY)
    applied, curvature_new = pl.pallas_call(
        kernel,
        out_shape=(
            pltpu.VMEM((OWN, NW), F32),
            pltpu.VMEM((KW, NW), BF16),
        ),
        in_specs=[hbm] * 5,
        out_specs=(pl.BlockSpec(memory_space=pltpu.VMEM),) * 2,
        scratch_shapes=[
            vm(inputs.shape, BF16), vm(out_grads.shape, BF16), vm(proj_in.shape, BF16),
            vm(proj_out.shape, BF16), vm((KP, NW), BF16),
            vm((8, FEATS, 128), BF16), vm((3, 2, ZR, 128), BF16), vm((2, ZR, 128), BF16),
            vm((NY, 4, ZR, 128), BF16), vm((7, YR, 128), BF16), vm((YR, 128), BF16),
            vm((3, YR, 128), BF16), vm((YR, 128), BF16), vm((FEATS, 512), BF16),
            vm((PIN, 512), F32), vm((256, 512), BF16), vm((256, 512), BF16),
            vm((16, PIN * POUT), BF16),
            vm((32, 16, NW), BF16), vm((32, 16, KP), BF16), vm((KP, 512), BF16),
            vm((32, 16, NW), BF16), vm((2, 4, 4, 16, NW), BF16),
            vm((4, 16, NW), BF16), vm((3, 16, NW), BF16),
            vm((16, 512), BF16), vm((16, 512), BF16), vm((7, 16, 512), BF16), vm((16, 512), BF16),
            dma((5,)), dma, dma, dma, dma, dma, dma, dma, dma, dma, dma, dma, dma, dma, dma,
            dma, dma((4,)), dma, dma((2, 4, 4)), dma, dma, dma, dma((3,)), dma, dma,
            dma, dma((2, 4, 4)), dma, dma, dma, dma, dma, dma,
        ],
        compiler_params=pltpu.CompilerParams(
            collective_id=0, has_side_effects=True, vmem_limit_bytes=48 * 2**20
        ),
    )(*(
        pltpu.with_memory_space_constraint(a, pltpu.HBM)
        for a in (inputs, out_grads, proj_in, proj_out, curvature)
    ))
    return pl.pallas_call(
        hand_over,
        out_shape=(
            jax.ShapeDtypeStruct((OWN, NW), F32),
            jax.ShapeDtypeStruct((KW, NW), BF16),
        ),
        in_specs=[hbm] * 2,
        out_specs=(hbm, hbm),
        scratch_shapes=[dma((5,))],
        compiler_params=pltpu.CompilerParams(vmem_limit_bytes=2 * 2**20),
    )(applied, curvature_new)


def solution(mesh):
    in_specs = (P("col", "hid"), P("col", "hid"), P(None, "hid"), P(None, "hid"), P("hid", "col"))
    out_specs = (P("hid", "col"), P("hid", "col"))
    return jax.shard_map(
        per_device, mesh=mesh, in_specs=in_specs, out_specs=out_specs, check_vma=False
    )
```

```python
import jax
import jax.numpy as jnp
from jax import lax
from jax.experimental import pallas as pl
from jax.experimental.pallas import tpu as pltpu
from jax.sharding import PartitionSpec as P

MESH = pl.DeviceIdType.MESH
F32 = jnp.float32
BF16 = jnp.bfloat16

PIN = 96
POUT = 192
FEATS = PIN + POUT
ZR = 112
YR = FEATS - ZR
SEQ = 32
EXAMPLES = 480
NY, NZ = 8, 4
N_HID, N_COL = 32, 16
OWN = 15
TOK = OWN * SEQ
NW = 1152
KW = 576
KP = 640
gram_weight = 1.0 / 64.0
apply_weight = 1.0 / 16.0
NT = (((1,), (1,)), ((), ()))


def slot_of(y, z):
    return (z // 2) * 16 + y * 2 + z % 2


def root_group(y, z):
    return (y + 16 - 4 * (z % 2) - 2 * (z // 2)) % NY


def block_slot(y, z):
    return slot_of(root_group(y, z), z)


def kernel(
    x_hbm, g_hbm, wi_hbm, wo_hbm, c_hbm,
    app_ref, cn_out,
    xv, gv, wiv, wov, cx,
    part, q1, qs, q2, r1, s1, r2, s2, r3, featv, ge, go, rows,
    rn, rk, rkt, p, rp, zs, zr, sp, sq, sr, sall,
    in_sem, q1s, q1r, q2s, q2r, a1s, a1r, a2s, a2r, a3s, a3r, ns, nr, ks, kr,
    zas, zar, yas, yar, khs, khr, kxs, kyr, kxr, kcs, kcr,
    rps, rpr, zrs, zrr, scs, scr, sms, smr,
):
    h = lax.axis_index("hid")
    c = lax.axis_index("col")
    y, z = h // NZ, h % NZ
    core = c % 2
    m = c // 2
    x, zh = m // 2, m % 2
    first_y = (m + 2 * core + NY - 1) % NY

    def chunk_of(yy):
        return (yy + NY - first_y) % NY

    z_target = 2 * core + chunk_of(y) // 4
    y_root = (m + 4 * (z % 2) + 2 * (z // 2)) % NY
    is_target = z == z_target
    is_root = jnp.logical_and(y == y_root, core == z // 2)
    own_slot = block_slot(y, z)

    def hid_dev(yy, zz):
        return (yy * NZ + zz, c)

    def col_dev(cc):
        return (h, cc)

    def send(src, dst, ssem, rsem, dev):
        copy = pltpu.make_async_remote_copy(
            src_ref=src, dst_ref=dst, send_sem=ssem, recv_sem=rsem,
            device_id=dev, device_id_type=MESH,
        )
        copy.start()

    def wait_for(ref, sem):
        pltpu.make_async_copy(ref, ref, sem).wait()

    off = pl.multiple_of(64 * (h % 2), 64)
    loads = []
    for i, (src, dst) in enumerate(
        (
            (x_hbm, xv), (wi_hbm, wiv), (g_hbm, gv), (wo_hbm, wov),
            (c_hbm, cx.at[pl.ds(off, KW)]),
        )
    ):
        load = pltpu.make_async_copy(src, dst, in_sem.at[i])
        load.start()
        loads.append(load)

    barrier = pltpu.get_barrier_semaphore()

    def greet(dev):
        pl.semaphore_signal(barrier, inc=1, device_id=dev, device_id_type=MESH)

    for d in range(1, NY):
        greet(hid_dev((y + d) % NY, z))
    for d in range(1, NZ):
        greet(hid_dev(y, (z + d) % NZ))
    zh_c = (x * 2 + (1 - zh)) * 2 + core
    greet(col_dev(zh_c))
    for d in range(1, 4):
        greet(col_dev((((x + d) % 4) * 2 + zh) * 2 + core))
    greet(col_dev(m * 2 + 1 - core))

    @pl.when(jnp.logical_not(is_root))
    def _():
        greet(col_dev(root_group(y, z) * 2 + z // 2))

    zero_tail = jnp.zeros((FEATS, 128), BF16)
    for hf in range(2):
        part[4 * hf + 3] = zero_tail
    loads[2].wait()
    loads[3].wait()

    def project(w, v, first):
        for hf in range(2):
            t = lax.dot_general(
                w[...], v[TOK * hf : TOK * (hf + 1), :], NT, preferred_element_type=F32
            ).astype(BF16)
            n = t.shape[0]
            for q in range(3):
                part[4 * hf + q, first : first + n, :] = t[:, 128 * q : 128 * (q + 1)]
            part[4 * hf + 3, first : first + n, 0:96] = t[:, 384:480]

    project(wov, gv, 0)
    loads[0].wait()
    loads[1].wait()
    project(wiv, xv, POUT)

    pl.semaphore_wait(barrier, jnp.where(is_root, 30, 15))

    z_first = pl.ds(0, ZR)
    y_first = pl.ds(ZR, YR)
    for d in (2, 1, 3):
        zz = (z + d) % NZ
        send(part.at[pl.ds(2 * zz, 2), z_first], q1.at[d - 1], q1s, q1r, hid_dev(y, zz))
    for d in (4, 3, 5, 2, 6, 1, 7):
        yy = (y + d) % NY
        send(part.at[chunk_of(yy), y_first], r1.at[d - 1], a1s, a1r, hid_dev(yy, z))
    cx[pl.ds(pl.multiple_of(KW * (1 - h % 2), 64), 64), :] = jnp.zeros((64, NW), BF16)

    wait_for(q1, q1r)
    both = part[pl.ds(2 * z, 2), 0:ZR].astype(F32)
    for d in range(3):
        both = both + q1[d].astype(F32)
    qs[...] = both.astype(BF16)
    q_z = 2 * core + z // 2
    q_y = (m + 4 * (z // 2) + 2 * core) % NY
    q_place = q2.at[y, pl.ds(2 * (z % 2), 2)]
    q_here = jnp.logical_and(q_y == y, q_z == z)

    @pl.when(q_here)
    def _():
        pltpu.make_async_copy(qs, q_place, q2r).start()

    @pl.when(jnp.logical_not(q_here))
    def _():
        send(qs, q_place, q2s, q2r, hid_dev(q_y, q_z))

    wait_for(r1, a1r)
    total = part[chunk_of(y), ZR:FEATS].astype(F32)
    for d in range(7):
        total = total + r1[d].astype(F32)
    s1[...] = total.astype(BF16)

    @pl.when(jnp.logical_not(is_target))
    def _():
        send(s1, r2.at[(z - z_target + NZ) % NZ - 1], a2s, a2r, hid_dev(y, z_target))
        wait_for(s1, a2s)

    @pl.when(is_target)
    def _():
        wait_for(r2, a2r)
        whole = s1[...].astype(F32)
        for d in range(3):
            whole = whole + r2[d].astype(F32)
        s2[...] = whole.astype(BF16)
        place = r3.at[y_first, pl.ds(pl.multiple_of(128 * (chunk_of(y) % 4), 128), 128)]

        @pl.when(y != y_root)
        def _():
            send(s2, place, a3s, a3r, hid_dev(y_root, z))
            wait_for(s2, a3s)

        @pl.when(y == y_root)
        def _():
            pltpu.make_async_copy(s2, place, a3r).start()

    @pl.when(jnp.logical_not(q_here))
    def _():
        wait_for(qs, q2s)

    k_base = core * 16 + m * 2

    @pl.when(is_root)
    def _():
        wait_for(q2, q2r)
        for t in range(4):
            summed = q2[0, t].astype(F32)
            for d in range(1, NY):
                summed = summed + q2[d, t].astype(F32)
            r3[0:ZR, 128 * t : 128 * (t + 1)] = summed.astype(BF16)
        wait_for(r3.at[y_first], a3r)
        ge[0:POUT, :] = r3[0:POUT, :]
        ge[POUT:256, :] = jnp.zeros((64, 512), BF16)
        go[0:64, :] = jnp.zeros((64, 512), BF16)
        go[64:256, :] = r3[0:POUT, :]
        featv[...] = r3[POUT:FEATS, :].astype(F32)
        mine = (
            lax.broadcasted_iota(jnp.int32, (16, 512), 1) // SEQ
            == lax.broadcasted_iota(jnp.int32, (16, 512), 0)
        )

        def n_slice(cc):
            return rows.at[:, pl.ds(pl.multiple_of(cc * NW, 128), NW)]

        def k_slice(kk):
            return rows.at[:, pl.ds(pl.multiple_of((kk // 2) * NW + (kk % 2) * 512, 128), KP)]

        def to_col(cc):
            @pl.when(cc != c)
            def _():
                send(n_slice(cc), rn.at[own_slot], ns, nr, col_dev(cc))

            @pl.when(cc == c)
            def _():
                pltpu.make_async_copy(n_slice(cc), rn.at[own_slot], nr).start()

        def to_hid(kk):
            @pl.when(kk != h)
            def _():
                send(k_slice(kk), rk.at[own_slot], ks, kr, (kk, c))

            @pl.when(kk == h)
            def _():
                pltpu.make_async_copy(k_slice(kk), rk.at[own_slot], kr).start()

        def form(step, carry):
            i = (x + 3 - step) % 4
            def spread(odd):
                return jnp.concatenate(
                    [
                        jnp.where(
                            mine,
                            jnp.broadcast_to(featv[pl.ds(i * 24 + 2 * q + odd, 1), :], (16, 512)),
                            0.0,
                        ).astype(BF16)
                        for q in range(12)
                    ],
                    axis=0,
                )

            even = lax.dot_general(spread(0), ge[...], NT, preferred_element_type=F32)
            odd = lax.dot_general(spread(1), go[...], NT, preferred_element_type=F32)
            for q in range(12):
                e = even[16 * q : 16 * (q + 1)]
                o = odd[16 * q : 16 * (q + 1)]
                three = jnp.concatenate(
                    [e[:, 0:128], e[:, 128:256] + o[:, 0:128], o[:, 128:256]], axis=1
                )
                at = pl.multiple_of(i * 4608 + 384 * q, 128)
                rows[:, pl.ds(at, 384)] = three.astype(BF16)
            for dc in range(2):
                to_col(4 * i + 2 * (1 - zh) + dc)
            for dk in range(8):
                to_hid(8 * i + dk)
            for dc in range(2):
                to_col(4 * i + 2 * zh + dc)
            return carry

        lax.fori_loop(0, 4, form, 0)

    up, down = (y + 1) % NY, (y + NY - 1) % NY

    def y_block(hop, way, j):
        yy = (y - hop + NY) % NY if way == 0 else (y + hop) % NY
        return rn.at[block_slot(yy, (z + j) % NZ)]

    def y_hops(way, j):
        return 4 if (j < 2) == (way == 0) else 3

    def y_send(hop, way, j):
        block = y_block(hop, way, j)
        send(block, block, yas, yar.at[way, hop, j], hid_dev(up if way == 0 else down, z))

    wait_for(rn.at[own_slot], nr)
    for way in range(2):
        y_send(0, way, 0)
    for d in range(1, NZ):
        send(rn.at[own_slot], rn.at[own_slot], zas, zar.at[NZ - d], hid_dev(y, (z + d) % NZ))
    wait_for(rk.at[pl.ds(k_base, 2)], kr)
    k_two = rk.at[pl.ds(k_base, 2)]
    send(k_two, k_two, khs, khr, col_dev(zh_c))

    def k_over_x(two, rsem):
        for d in range(1, 4):
            to = (((x + d) % 4) * 2 + zh) * 2 + core
            send(two, two, kxs, rsem.at[d - 1], col_dev(to))

    k_over_x(k_two, kyr)
    for j in range(1, NZ):
        wait_for(rn.at[block_slot(y, (z + j) % NZ)], zar.at[j])
        for way in range(2):
            y_send(0, way, j)

    def y_round(hop):
        for j in range(NZ):
            for way in range(2):
                if hop <= y_hops(way, j):
                    wait_for(y_block(hop, way, j), yar.at[way, hop - 1, j])
                    if hop < y_hops(way, j):
                        y_send(hop, way, j)

    def p_slot(left_hops, way, j):
        yy = (y + left_hops) % NY if way == 0 else (y - left_hops + NY) % NY
        return slot_of(yy, (2 * core + j) % NZ)

    def p_round(step, which=range(NZ)):
        for j in which:
            for way in range(2):
                hops = y_hops(way, j)
                left = 4 - step
                if left > hops:
                    continue
                at = p_slot(left, way, j)
                if left == hops:
                    src = p.at[at]
                else:
                    src = rp.at[way, step - 1, j]
                    wait_for(src, rpr.at[way, step - 1, j])
                    src[...] = (src[...].astype(F32) + p[at].astype(F32)).astype(BF16)
                send(src, rp.at[way, step, j], rps, rpr.at[way, step, j],
                     hid_dev(up if way == 0 else down, z))

    k_other = rk.at[pl.ds(core * 16 + x * 4 + (1 - zh) * 2, 2)]
    wait_for(k_other, khr)
    k_over_x(k_other, kxr)
    y_round(1)
    for d in range(1, 4):
        at = core * 16 + ((x + 4 - d) % 4) * 4
        wait_for(rk.at[pl.ds(at + zh * 2, 2)], kyr.at[d - 1])
        wait_for(rk.at[pl.ds(at + (1 - zh) * 2, 2)], kxr.at[d - 1])
    k_all = rk.at[pl.ds(core * 16, 16)]
    send(k_all, k_all, kcs, kcr, col_dev(m * 2 + 1 - core))
    y_round(2)
    loads[4].wait()

    def product(half):
        for b in range(2):
            at = pl.ds(half * 16 + 8 * b, 8)
            prod = jnp.dot(
                rk[at].reshape(128, KP), cx[...], preferred_element_type=F32
            )
            p[at] = (prod * apply_weight).astype(BF16).reshape(8, 16, NW)

    product(core)
    p_round(0, (0, 1))
    wait_for(rk.at[pl.ds((1 - core) * 16, 16)], kcr)
    product(1 - core)
    p_round(0, (2, 3))
    y_round(3)
    p_round(1)
    y_round(4)

    sp[...] = lax.dot_general(
        rn[slot_of(y, z)], rn[...].reshape(512, NW), NT, preferred_element_type=F32
    ).astype(BF16)
    send(sp, sq, scs, scr, col_dev(m * 2 + 1 - core))
    p_round(2)
    wait_for(sq, scr)
    sall[...] = (sp[...].astype(F32) + sq[...].astype(F32)).astype(BF16)
    for d in range(1, 8):
        send(sall, sr.at[d - 1], sms, smr, col_dev(((m + d) % 8) * 2 + core))

    p_round(3)

    rkt[...] = rk[...].reshape(512, KP).T
    factor = gram_weight / EXAMPLES
    for b in range(3):
        lines = pl.ds(pl.multiple_of(off + 192 * b, 64), 192)
        left = rkt[lines, :]
        for n in range(3):
            cols = slice(384 * n, 384 * (n + 1))
            gram = jnp.dot(left, rn[:, :, cols].reshape(512, 384), preferred_element_type=F32)
            new = cx[lines, cols].astype(F32) + gram * factor
            cn_out[192 * b : 192 * (b + 1), cols] = new.astype(BF16)

    for j in range(NZ):
        zz = (2 * core + j) % NZ
        for way in range(2):
            wait_for(rp.at[way, 3, j], rpr.at[way, 3, j])
        done = p[slot_of(y, zz)].astype(F32)
        for way in range(2):
            done = done + rp[way, 3, j].astype(F32)
        zs[j] = done.astype(BF16)

        @pl.when(z != zz)
        def _():
            send(zs.at[j], zr.at[(zz - z + NZ) % NZ - 1], zrs, zrr, hid_dev(y, zz))

    wait_for(sr, smr)
    s = sall[...].astype(F32)
    for d in range(7):
        s = s + sr[d].astype(F32)
    high = s.astype(BF16)
    low = (s - high.astype(F32)).astype(BF16)
    both = jnp.dot(
        jnp.concatenate([high, low], axis=0), rn[...].reshape(512, NW),
        preferred_element_type=F32,
    )
    final = (both[0:16] + both[16:32]) * (factor * apply_weight) + zs[(z + NZ - 2 * core) % NZ].astype(F32)
    wait_for(zr, zrr)
    for d in range(3):
        final = final + zr[d].astype(F32)
    app_ref[...] = final[0:OWN, :]

    wait_for(q1, q1s)
    wait_for(r1, a1s)
    wait_for(rn.at[pl.ds(0, 3)], zas)
    wait_for(rn.at[pl.ds(0, 28)], yas)
    wait_for(rk.at[pl.ds(0, 2)], khs)
    wait_for(rk.at[pl.ds(0, 12)], kxs)
    wait_for(rk.at[pl.ds(0, 16)], kcs)
    wait_for(rn.at[pl.ds(0, 28)], rps)
    wait_for(zr, zrs)
    wait_for(sp, scs)
    wait_for(sr, sms)

    @pl.when(is_root)
    def _():
        wait_for(rn.at[pl.ds(0, 15)], ns)
        wait_for(rk.at[pl.ds(0, 31)], ks)


def hand_over(app_in, cn_in, app_out, cn_out, sem):
    copies = [pltpu.make_async_copy(app_in, app_out, sem.at[4])]
    for i in range(4):
        lines = pl.ds(144 * i, 144)
        copies.append(pltpu.make_async_copy(cn_in.at[lines], cn_out.at[lines], sem.at[i]))
    for copy in copies:
        copy.start()
    for copy in copies:
        copy.wait()


def per_device(inputs, out_grads, proj_in, proj_out, curvature):
    dma = pltpu.SemaphoreType.DMA
    vm = pltpu.VMEM
    hbm = pl.BlockSpec(memory_space=pl.ANY)
    applied, curvature_new = pl.pallas_call(
        kernel,
        out_shape=(
            pltpu.VMEM((OWN, NW), F32),
            pltpu.VMEM((KW, NW), BF16),
        ),
        in_specs=[hbm] * 5,
        out_specs=(pl.BlockSpec(memory_space=pltpu.VMEM),) * 2,
        scratch_shapes=[
            vm(inputs.shape, BF16), vm(out_grads.shape, BF16), vm(proj_in.shape, BF16),
            vm(proj_out.shape, BF16), vm((KP, NW), BF16),
            vm((8, FEATS, 128), BF16), vm((3, 2, ZR, 128), BF16), vm((2, ZR, 128), BF16),
            vm((NY, 4, ZR, 128), BF16), vm((7, YR, 128), BF16), vm((YR, 128), BF16),
            vm((3, YR, 128), BF16), vm((YR, 128), BF16), vm((FEATS, 512), BF16),
            vm((PIN, 512), F32), vm((256, 512), BF16), vm((256, 512), BF16),
            vm((16, PIN * POUT), BF16),
            vm((32, 16, NW), BF16), vm((32, 16, KP), BF16), vm((KP, 512), BF16),
            vm((32, 16, NW), BF16), vm((2, 4, 4, 16, NW), BF16),
            vm((4, 16, NW), BF16), vm((3, 16, NW), BF16),
            vm((16, 512), BF16), vm((16, 512), BF16), vm((7, 16, 512), BF16), vm((16, 512), BF16),
            dma((5,)), dma, dma, dma, dma, dma, dma, dma, dma, dma, dma, dma, dma, dma, dma,
            dma, dma((4,)), dma, dma((2, 4, 4)), dma, dma, dma, dma((3,)), dma((3,)), dma, dma,
            dma, dma((2, 4, 4)), dma, dma, dma, dma, dma, dma,
        ],
        compiler_params=pltpu.CompilerParams(
            collective_id=0, has_side_effects=True, vmem_limit_bytes=48 * 2**20
        ),
    )(*(
        pltpu.with_memory_space_constraint(a, pltpu.HBM)
        for a in (inputs, out_grads, proj_in, proj_out, curvature)
    ))
    return pl.pallas_call(
        hand_over,
        out_shape=(
            jax.ShapeDtypeStruct((OWN, NW), F32),
            jax.ShapeDtypeStruct((KW, NW), BF16),
        ),
        in_specs=[hbm] * 2,
        out_specs=(hbm, hbm),
        scratch_shapes=[dma((5,))],
        compiler_params=pltpu.CompilerParams(vmem_limit_bytes=2 * 2**20),
    )(applied, curvature_new)


def solution(mesh):
    in_specs = (P("col", "hid"), P("col", "hid"), P(None, "hid"), P(None, "hid"), P("hid", "col"))
    out_specs = (P("hid", "col"), P("hid", "col"))
    return jax.shard_map(
        per_device, mesh=mesh, in_specs=in_specs, out_specs=out_specs, check_vma=False
    )
```
